256 devices in a mesh: ctx: 128 (over x, y_lo, z, core), tp: 2 (over y_hi).
Axes of the slice: x: 4, y: 4 (y_hi: 2, y_lo: 2; y = y_hi * 2 + y_lo), z: 8, core: 2. Of those that a mesh axis runs over, the one named last changes fastest.
Arguments:
- query_rows: bfloat16 [16384, 8192], P('ctx', 'tp'), may hold values from -6 to 6
- key_rows: bfloat16 [16384, 8192], P('ctx', 'tp'), may hold values from -6 to 6
- value_rows: bfloat16 [16384, 8192], P('ctx', 'tp'), may hold values from -6 to 6
- decay_rate: float32 [8, 8192], P(None, 'tp'), may hold values from 6.1035157e-06 to 0.05
- residue: float32 [8, 8192], P(None, 'tp'), may hold values from -1.5 to 1.5
- norm_gain: float32 [8192], P('tp'), may hold values from 0.5 to 1.5
- grad_out: bfloat16 [16384, 8192], P('ctx', 'tp'), may hold values from -6 to 6
Outputs:
- normed_out: bfloat16 [16384, 8192], P('ctx', 'tp')
- grad_query: bfloat16 [16384, 8192], P('ctx', 'tp')
- grad_key: bfloat16 [16384, 8192], P('ctx', 'tp')
- grad_value: bfloat16 [16384, 8192], P('ctx', 'tp')
- grad_residue: float32 [8, 8192], P(None, 'tp')
The draws below stay inside these ranges and needn't reach their ends.
All inputs are finite; a program needn't handle non-finite values.
Results may differ from the reference program's by a relative error of at most 0.0029.
Values sent between devices are 32-bit elements; how exact they have to be, the bound alone decides.
No kernel may reach another device: no remote copies, remote signals or barrier semaphores. Data moves between devices by JAX's collectives and lax.ppermute only.
A program may use at most 192 MiB of HBM per device.

```python
import math
import jax
import jax.numpy as jnp
from jax import lax

D = 8192
MODES = 8
TOK_DEV = 128
TOKENS = 16384


def stretch_levels(key, lower, upper):
    level_key = jax.random.fold_in(key, 101)
    exponents = jax.random.uniform(level_key, (TOKENS // TOK_DEV,), jnp.float32, lower, upper)
    return jnp.repeat(jnp.exp(exponents), TOK_DEV)[:, None]


def draw_key_rows(key, part):
    levels = stretch_levels(key, -4.0, 0.4)
    key = jax.random.fold_in(key, 3)
    base_values = jax.random.truncated_normal(key, -4.0, 4.0, (TOKENS, D), jnp.float32)
    return (base_values * levels).astype(jnp.bfloat16)


def draw_grad_out(key, part):
    levels = stretch_levels(key, -4.0, 0.4)
    key = jax.random.fold_in(key, 5)
    base_values = jax.random.truncated_normal(key, -4.0, 4.0, (TOKENS, D), jnp.float32)
    return (base_values * levels).astype(jnp.bfloat16)


def steps_of(key, extent, cuts, least, largest):
    def one(dim, shards_of):
        draws = jax.random.uniform(jax.random.fold_in(jax.random.fold_in(key, 6), dim), (shards_of,), jnp.float32, least / len(cuts), largest / len(cuts))
        return jnp.repeat(jnp.exp(draws), extent[dim] // shards_of).reshape((-1,) + (1,) * (len(extent) - dim - 1))

    level = one(*cuts[0])
    for cut in cuts[1:]:
        level = level * one(*cut)
    return level


def centred(key, shape, spread, reach, cuts=(), held_as=jnp.bfloat16):
    array = spread * jax.random.normal(key, shape, jnp.float32)
    if cuts:
        array = array * steps_of(key, shape, cuts, -0.22, 0.18)
    return jnp.clip(array, -reach, reach).astype(held_as)


def setup_inputs(seed: int = 0) -> dict:
    streams_of = jax.random.split(jax.random.key(seed), 8)
    return {
        "query_rows": centred(streams_of[0], (TOKENS, D), 1.0, 6.0, ((0, 128), (1, 2))),
        "key_rows": draw_key_rows(jax.random.fold_in(streams_of[7], 71), 0),
        "value_rows": centred(streams_of[2], (TOKENS, D), 1.0, 6.0, ((0, 128), (1, 2))),
        "decay_rate": jnp.clip(jnp.exp(math.log(0.05) - 9.010913 * jax.random.uniform(streams_of[3], (MODES, D), jnp.float32) ** steps_of(streams_of[3], (MODES, D), ((1, 2),), -0.2, 0.2)), 6.10351571594947e-06, 0.05),
        "residue": centred(streams_of[4], (MODES, D), 0.25, 1.5, ((1, 2),), jnp.float32),
        "norm_gain": jnp.clip(1.0 + 0.1 * jax.random.normal(streams_of[5], (D,), jnp.float32), 0.5, 1.5),
        "grad_out": draw_grad_out(jax.random.fold_in(streams_of[7], 71), 0),
    }


channel_block = 512
norm_eps = 1e-05

def modal_filter(product_in, decay_part, residue_part):
    retention = jnp.exp(-decay_part)
    in_scale = jnp.sqrt(-jnp.expm1(-2.0 * decay_part))

    def advance(carried, row_in):
        carried = retention * carried + in_scale * row_in[None, :]
        return (carried, lax.optimization_barrier(jnp.sum(residue_part * carried, axis=0)))
    _, filtered = lax.scan(advance, jnp.zeros_like(decay_part), product_in)
    return filtered

def modal_adjoint(product_in, grad_filtered, decay_part, residue_part):
    retention = jnp.exp(-decay_part)
    in_scale = jnp.sqrt(-jnp.expm1(-2.0 * decay_part))
    zeros_modal = jnp.zeros_like(decay_part)

    def forward_step(carried, rows_both):
        modal_now, running = carried
        row_in, row_grad = rows_both
        modal_now = retention * modal_now + in_scale * row_in[None, :]
        running = running + row_grad[None, :] * modal_now
        return ((modal_now, running), None)
    (_, grad_residue), _ = lax.scan(forward_step, (zeros_modal, zeros_modal), (product_in, grad_filtered))

    def backward_step(adjoint, row_grad):
        adjoint = retention * adjoint + row_grad[None, :]
        return (adjoint, lax.optimization_barrier(jnp.sum(in_scale * residue_part * adjoint, axis=0)))
    _, grad_product = lax.scan(backward_step, zeros_modal, grad_filtered, reverse=True)
    return (grad_residue, grad_product)

def join_blocks(stacked):
    moved_axes = jnp.moveaxis(stacked, 0, -2)
    return moved_axes.reshape(moved_axes.shape[:-2] + (moved_axes.shape[-2] * moved_axes.shape[-1],))

def reference(query_rows, key_rows, value_rows, decay_rate, residue, norm_gain, grad_out):
    block_width = min(channel_block, D)
    block_count = D // block_width

    def block_pieces(block_index):
        first_col = (block_index * block_width).astype(jnp.int32)

        def take_block(source):
            return lax.dynamic_slice_in_dim(source, first_col, block_width, source.ndim - 1)
        query_part = take_block(query_rows).astype(jnp.float32)
        key_part = take_block(key_rows).astype(jnp.float32)
        value_part = take_block(value_rows).astype(jnp.float32)
        grad_part = take_block(grad_out).astype(jnp.float32)
        return (query_part, key_part, value_part, take_block(decay_rate), take_block(residue), take_block(norm_gain), grad_part)

    def gather_sums(carried, block_index):
        squares, dot_sums = carried
        query_part, key_part, value_part, decay_part, residue_part, gain_part, grad_part = block_pieces(block_index)
        filtered = modal_filter(key_part * value_part, decay_part, residue_part)
        gated = query_part * filtered
        weighted = gain_part[None, :] * grad_part
        return ((squares + lax.optimization_barrier(jnp.sum(gated * gated, axis=1)), dot_sums + lax.optimization_barrier(jnp.sum(weighted * gated, axis=1))), None)
    zeros_tokens = jnp.zeros((TOKENS,), jnp.float32)
    indices = jnp.arange(block_count, dtype=jnp.int32)
    (squares, dot_sums), _ = lax.scan(gather_sums, (zeros_tokens, zeros_tokens), indices)
    rms_scale = jnp.sqrt(squares / D + norm_eps)

    def finish(carried, block_index):
        query_part, key_part, value_part, decay_part, residue_part, gain_part, grad_part = block_pieces(block_index)
        product_in = key_part * value_part
        filtered = modal_filter(product_in, decay_part, residue_part)
        gated = query_part * filtered
        normed = (gated * gain_part[None, :] / rms_scale[:, None]).astype(jnp.bfloat16)
        grad_gated = gain_part[None, :] * grad_part / rms_scale[:, None] - gated * (dot_sums / (D * rms_scale ** 3))[:, None]
        grad_filtered = grad_gated * query_part
        grad_residue, grad_product = modal_adjoint(product_in, grad_filtered, decay_part, residue_part)
        results = (normed, (grad_gated * filtered).astype(jnp.bfloat16), (grad_product * value_part).astype(jnp.bfloat16), (grad_product * key_part).astype(jnp.bfloat16), grad_residue)
        return (carried, results)
    _, results = lax.scan(finish, jnp.zeros((), jnp.float32), indices)
    normed_out, grad_query, grad_key, grad_value, grad_residue = results
    return (join_blocks(normed_out), join_blocks(grad_query), join_blocks(grad_key), join_blocks(grad_value), join_blocks(grad_residue))
```

```python
import functools

import jax
import jax.numpy as jnp
from jax import lax
from jax.experimental import pallas as pl
from jax.experimental.pallas import tpu as pltpu
from jax.sharding import Mesh, PartitionSpec as P

D = 8192
MODES = 8
norm_eps = 1e-05

LANES = 128
SUB = 8
ROWS16 = 16

CHIP_AXES = ("x", "yl", "z")
CTX_AXES = CHIP_AXES + ("core",)
CTX_SIZES = (4, 2, 8, 2)

f32 = jnp.float32
bf16 = jnp.bfloat16


def call(body, out_shape, *args, scratch=()):
    vmem = pl.BlockSpec(memory_space=pltpu.VMEM)
    return pl.pallas_call(
        body,
        out_shape=out_shape,
        in_specs=[vmem] * len(args),
        out_specs=jax.tree.map(lambda _: vmem, out_shape),
        scratch_shapes=list(scratch),
        compiler_params=pltpu.CompilerParams(vmem_limit_bytes=48 * 1024 * 1024),
    )(*args)


def shaped(*extent, dtype=f32):
    return jax.ShapeDtypeStruct(extent, dtype)


def dense_rows(group, first, tokens):
    return pl.ds(((group // SUB) * tokens + first) * SUB + group % SUB, SUB, stride=SUB)


def each_tile(tokens, groups, body, start=None, finish=None):
    def rows(tile, nothing):
        first = pl.multiple_of(tile * ROWS16, ROWS16)
        carried = start() if start else None
        for group in range(groups):
            carried = body(first, group, carried)
        if finish:
            finish(first, carried)
        return nothing

    lax.fori_loop(0, tokens // ROWS16, rows, 0)


def load_dense(ref, group, first, tokens):
    return jnp.concatenate(
        [ref[dense_rows(group, first + shift, tokens), :] for shift in (0, SUB)], axis=0
    )


def store_dense(ref, group, first, tokens, value):
    for shift in (0, SUB):
        ref[dense_rows(group, first + shift, tokens), :] = value[shift : shift + SUB]


def lanes_of(group):
    return pl.ds(group * LANES, LANES)


def tile_of(ref, first, group):
    return ref[pl.ds(first, ROWS16), lanes_of(group)].astype(f32)


def modes_of(ref, block, groups):
    return [ref[pl.ds(mode * groups + block * SUB, SUB), :] for mode in range(MODES)]


def put_modes(ref, block, groups, values):
    for mode in range(MODES):
        ref[pl.ds(mode * groups + block * SUB, SUB), :] = values[mode]


def tree_sum(terms):
    while len(terms) > 1:
        terms = [a + b for a, b in zip(terms[::2], terms[1::2])]
    return terms[0]


UNROLL = 8


def over_tokens(tokens, step, carried, backward=False):
    def several(turn, carried):
        for inner in range(UNROLL):
            at = turn * UNROLL + inner
            carried = step(tokens - 1 - at if backward else at, carried)
        return carried

    return lax.fori_loop(0, tokens // UNROLL, several, carried)


def token_row(block, token, tokens):
    return pl.ds(pl.multiple_of((block * tokens + token) * SUB, SUB), SUB)


def local_ends(tokens, groups, key, value, decay, scale, residue, product, keep, send, shrink, weight, scale_dense, whole, ends):
    for group in range(groups):
        rows = pl.ds(group, MODES, stride=groups)
        rate = decay[:, lanes_of(group)]
        in_scale = scale[:, lanes_of(group)]
        shrink[rows, :] = jnp.exp(-rate)
        whole[rows, :] = jnp.exp(-rate * tokens)
        scale_dense[rows, :] = in_scale
        weight[rows, :] = in_scale * residue[:, lanes_of(group)]

    def multiply(first, group, carried):
        store_dense(product, group, first, tokens, tile_of(key, first, group) * tile_of(value, first, group))

    each_tile(tokens, groups, multiply)
    blocks = groups // SUB
    for block in range(blocks):
        ratio = modes_of(shrink, block, groups)

        def step(token, states):
            row = product[token_row(block, token, tokens), :]
            return [r * s + row for r, s in zip(ratio, states)]

        zeros = [jnp.zeros((SUB, LANES), f32)] * MODES
        put_modes(ends, block, groups, over_tokens(tokens, step, zeros))
    core = lax.axis_index("core")
    half = MODES * groups // 2
    keep[...] = ends[pl.ds(pl.multiple_of(core * half, half), half), :]
    send[...] = ends[pl.ds(pl.multiple_of((1 - core) * half, half), half), :]


def my_half(ref, half):
    return ref[pl.ds(pl.multiple_of(lax.axis_index("core") * half, half), half), :]


def chip_total(backward, half, whole, keep, recv, total):
    core = lax.axis_index("core")
    mine_is_farther = core == (1 if backward else 0)
    mine, other = keep[...], recv[...]
    farther = jnp.where(mine_is_farther, mine, other)
    nearer = jnp.where(mine_is_farther, other, mine)
    total[...] = my_half(whole, half) * farther + nearer


def chip_scan(backward, chips, whole_cut, totals, before):
    position = lax.axis_index(CHIP_AXES)
    core = lax.axis_index("core")
    ratio = whole_cut[core * chips + position]
    ratio = ratio * ratio

    def step(turn, state):
        at = chips - 1 - turn if backward else turn
        before[at] = state
        return ratio * state + totals[at]

    lax.fori_loop(0, chips, step, jnp.zeros_like(ratio), unroll=8)


def chip_scan_and_sum(chips, whole_cut, totals, before):
    position = lax.axis_index(CHIP_AXES)
    core = lax.axis_index("core")
    ratio = whole_cut[core * chips + position]
    ratio = ratio * ratio

    def step(turn, carried):
        state, total = carried
        at = chips - 1 - turn
        before[at, 0] = state
        return ratio * state + totals[at, 0], total + totals[at, 1]

    zero = jnp.zeros_like(ratio)
    _, total = lax.fori_loop(0, chips, step, (zero, zero), unroll=8)
    before[:, 1] = jnp.broadcast_to(total[None], before[:, 1].shape)


def core_states(backward, half, whole, chip_state, keep, recv, mine, other):
    core = lax.axis_index("core")
    mine_is_farther = core == (1 if backward else 0)
    farther = jnp.where(mine_is_farther, keep[...], recv[...])
    first = chip_state[...]
    second = my_half(whole, half) * first + farther
    mine[...] = jnp.where(mine_is_farther, first, second)
    other[...] = jnp.where(mine_is_farther, second, first)


def join_halves(ref, half, mine, other):
    core = lax.axis_index("core")
    ref[pl.ds(pl.multiple_of(core * half, half), half), :] = mine
    ref[pl.ds(pl.multiple_of((1 - core) * half, half), half), :] = other


def filter_rows(tokens, groups, product, shrink, weight, entry_mine, entry_other, query, grad, gain, filtered, sums, entry, squares, dots):
    join_halves(entry, MODES * groups // 2, entry_mine[...], entry_other[...])
    for block in range(groups // SUB):
        ratio = modes_of(shrink, block, groups)
        factor = modes_of(weight, block, groups)

        def step(token, states):
            at = token_row(block, token, tokens)
            row = product[at, :]
            states = [r * s + row for r, s in zip(ratio, states)]
            filtered[at, :] = tree_sum([w * s for w, s in zip(factor, states)])
            return states

        over_tokens(tokens, step, modes_of(entry, block, groups))

    def add(first, group, carried):
        gated = tile_of(query, first, group) * load_dense(filtered, group, first, tokens)
        weighted = gain[:, lanes_of(group)] * tile_of(grad, first, group)
        return carried[0] + gated * gated, carried[1] + weighted * gated

    def zeros():
        zero = jnp.zeros((ROWS16, LANES), f32)
        return zero, zero

    def keep(first, carried):
        squares[pl.ds(first, ROWS16), :] = carried[0]
        dots[pl.ds(first, ROWS16), :] = carried[1]

    each_tile(tokens, groups, add, zeros, keep)
    sums[0:1, :] = jnp.sum(squares[...].T, axis=0, keepdims=True)
    sums[1:2, :] = jnp.sum(dots[...].T, axis=0, keepdims=True)


def norm_and_adjoint(tokens, groups, sums, other_sums, filtered, product, shrink, weight, scale_dense, entry_mine, entry_other, query, grad, gain,
                     normed, grad_query, grad_product, keep, send, entry, inverse, slope, grad_filtered, leading, residue_term):
    join_halves(entry, MODES * groups // 2, entry_mine[...], entry_other[...])
    both = sums[...] + other_sums[...]
    rms = jnp.sqrt(both[0:1] / D + norm_eps)
    inverse[...] = jnp.broadcast_to(1.0 / rms, (LANES, tokens)).T
    slope[...] = jnp.broadcast_to(both[1:2] / (D * rms * rms * rms), (LANES, tokens)).T

    def finish(first, group, carried):
        rows = pl.ds(first, ROWS16)
        part = load_dense(filtered, group, first, tokens)
        asked = tile_of(query, first, group)
        gated = asked * part
        gains = gain[:, lanes_of(group)]
        scale = inverse[rows, :]
        normed[rows, lanes_of(group)] = (gated * gains * scale).astype(bf16)
        grad_gated = gains * tile_of(grad, first, group) * scale - gated * slope[rows, :]
        grad_query[rows, lanes_of(group)] = (grad_gated * part).astype(bf16)
        store_dense(grad_filtered, group, first, tokens, grad_gated * asked)

    each_tile(tokens, groups, finish)
    for block in range(groups // SUB):
        ratio = modes_of(shrink, block, groups)
        factor = modes_of(weight, block, groups)

        def step(token, carried):
            states, terms = carried
            at = token_row(block, token, tokens)
            row = grad_filtered[at, :]
            put_in = product[at, :]
            states = [r * s + row for r, s in zip(ratio, states)]
            terms = [q + put_in * s for q, s in zip(terms, states)]
            grad_product[at, :] = tree_sum([w * s for w, s in zip(factor, states)])
            return states, terms

        zeros = [jnp.zeros((SUB, LANES), f32)] * MODES
        states, terms = over_tokens(tokens, step, (zeros, zeros), backward=True)
        put_modes(leading, block, groups, states)
        put_modes(
            residue_term,
            block,
            groups,
            [
                i * (q + r * s * e)
                for i, q, r, s, e in zip(
                    modes_of(scale_dense, block, groups), terms, ratio, states, modes_of(entry, block, groups)
                )
            ],
        )
    half = MODES * groups // 2
    core = lax.axis_index("core")
    mine = pl.ds(pl.multiple_of(core * half, half), half)
    other = pl.ds(pl.multiple_of((1 - core) * half, half), half)
    keep[0], keep[1] = leading[mine, :], residue_term[mine, :]
    send[0], send[1] = leading[other, :], residue_term[other, :]


def chip_total_and_sum(half, chips, whole, keep, recv, total):
    core = lax.axis_index("core")
    mine, other = keep[0], recv[0]
    farther = jnp.where(core == 1, mine, other)
    nearer = jnp.where(core == 1, other, mine)
    cut = half // chips
    total[:, 0] = (my_half(whole, half) * farther + nearer).reshape(chips, cut, LANES)
    total[:, 1] = (keep[1] + recv[1]).reshape(chips, cut, LANES)


def core_states_and_sum(half, chips, whole, chip_state, keep, recv, mine, other):
    core = lax.axis_index("core")
    farther = jnp.where(core == 1, keep[0], recv[0])
    first = chip_state[:, 0].reshape(half, LANES)
    second = my_half(whole, half) * first + farther
    mine[0] = jnp.where(core == 1, first, second)
    other[0] = jnp.where(core == 1, second, first)
    summed = chip_state[:, 1].reshape(half, LANES)
    mine[1] = summed
    other[1] = summed


def grad_rows(tokens, groups, grad_product, shrink, weight, after_mine, after_other, key, value, grad_key, grad_value, grad_residue, after, total, dense):
    half = MODES * groups // 2
    join_halves(after, half, after_mine[0], after_other[0])
    join_halves(total, half, after_mine[1], after_other[1])
    for group in range(groups):
        grad_residue[:, lanes_of(group)] = total[pl.ds(group, MODES, stride=groups), :]
    for block in range(groups // SUB):
        ratio = modes_of(shrink, block, groups)

        def step(token, states):
            at = token_row(block, token, tokens)
            states = [r * s for r, s in zip(ratio, states)]
            dense[at, :] = tree_sum(states) + grad_product[at, :]
            return states

        start = [w * a for w, a in zip(modes_of(weight, block, groups), modes_of(after, block, groups))]
        over_tokens(tokens, step, start, backward=True)

    def finish(first, group, carried):
        rows = pl.ds(first, ROWS16)
        part = load_dense(dense, group, first, tokens)
        grad_key[rows, lanes_of(group)] = (part * tile_of(value, first, group)).astype(bf16)
        grad_value[rows, lanes_of(group)] = (part * tile_of(key, first, group)).astype(bf16)

    each_tile(tokens, groups, finish)


def swap(value, axis):
    return lax.ppermute(value, axis, [(0, 1), (1, 0)])


def on_device(query_rows, key_rows, value_rows, decay_rate, residue, norm_gain, grad_out):
    tokens, channels = query_rows.shape
    groups = channels // LANES
    rows = MODES * groups
    half = rows // 2
    chips = lax.axis_size(CHIP_AXES)
    cut = half // chips
    gain = norm_gain[None, :]
    in_scale = jnp.sqrt(-jnp.expm1(-2.0 * decay_rate))
    dense = shaped(tokens * groups, LANES)
    modal = shaped(rows, LANES)
    halved = shaped(half, LANES)
    two_halves = shaped(2, half, LANES)
    modal_scratch = pltpu.VMEM((rows, LANES), f32)
    square_scratch = pltpu.VMEM((tokens, LANES), f32)
    dense_scratch = pltpu.VMEM((tokens * groups, LANES), f32)
    bind = functools.partial

    product, keep, send, shrink, weight, scale_dense, whole = call(
        bind(local_ends, tokens, groups),
        (dense, halved, halved, modal, modal, modal, modal),
        key_rows, value_rows, decay_rate, in_scale, residue,
        scratch=[modal_scratch],
    )
    whole_cut = whole.reshape(2 * chips, cut, LANES)
    recv = swap(send, "core")
    total = call(bind(chip_total, False, half), halved, whole, keep, recv)
    totals = lax.all_to_all(total.reshape(chips, cut, LANES), CHIP_AXES, 0, 0)
    before = call(bind(chip_scan, False, chips), shaped(chips, cut, LANES), whole_cut, totals)
    chip_state = lax.all_to_all(before, CHIP_AXES, 0, 0).reshape(half, LANES)
    entry_mine, entry_send = call(bind(core_states, False, half), (halved, halved), whole, chip_state, keep, recv)
    entry_other = swap(entry_send, "core")

    filtered, sums = call(
        bind(filter_rows, tokens, groups),
        (dense, shaped(2, tokens)),
        product, shrink, weight, entry_mine, entry_other, query_rows, grad_out, gain,
        scratch=[modal_scratch, square_scratch, square_scratch],
    )
    other_sums = swap(sums, "tp")

    normed_out, grad_query, grad_product, keep, send = call(
        bind(norm_and_adjoint, tokens, groups),
        (shaped(tokens, channels, dtype=bf16), shaped(tokens, channels, dtype=bf16), dense, two_halves, two_halves),
        sums, other_sums, filtered, product, shrink, weight, scale_dense, entry_mine, entry_other, query_rows, grad_out, gain,
        scratch=[modal_scratch, square_scratch, square_scratch, dense_scratch, modal_scratch, modal_scratch],
    )
    recv = swap(send, "core")
    total = call(bind(chip_total_and_sum, half, chips), shaped(chips, 2, cut, LANES), whole, keep, recv)
    totals = lax.all_to_all(total, CHIP_AXES, 0, 0)
    before = call(bind(chip_scan_and_sum, chips), shaped(chips, 2, cut, LANES), whole_cut, totals)
    chip_state = lax.all_to_all(before, CHIP_AXES, 0, 0)
    after_mine, after_send = call(
        bind(core_states_and_sum, half, chips), (two_halves, two_halves), whole, chip_state, keep, recv
    )
    after_other = swap(after_send, "core")

    grad_key, grad_value, grad_residue = call(
        bind(grad_rows, tokens, groups),
        (shaped(tokens, channels, dtype=bf16), shaped(tokens, channels, dtype=bf16), shaped(MODES, channels)),
        grad_product, shrink, weight, after_mine, after_other, key_rows, value_rows,
        scratch=[modal_scratch, modal_scratch, dense_scratch],
    )
    return (normed_out, grad_query, grad_key, grad_value, grad_residue)


def solution(mesh):
    devices = mesh.devices
    cut_mesh = Mesh(devices.reshape(CTX_SIZES + (devices.shape[1],)), CTX_AXES + ("tp",))
    token_split = P(CTX_AXES, "tp")
    return jax.shard_map(
        on_device,
        mesh=cut_mesh,
        in_specs=(token_split, token_split, token_split, P(None, "tp"), P(None, "tp"), P("tp"), token_split),
        out_specs=(token_split, token_split, token_split, token_split, P(None, "tp")),
        check_vma=False,
    )
```

```python
import functools

import jax
import jax.numpy as jnp
from jax import lax
from jax.experimental import pallas as pl
from jax.experimental.pallas import tpu as pltpu
from jax.sharding import Mesh, PartitionSpec as P

D = 8192
MODES = 8
HALF_MODES = MODES // 2
norm_eps = 1e-05

LANES = 128
SUB = 8
ROWS16 = 16
UNROLL = 8
CHUNKS = 4

CHIP_AXES = ("x", "yl", "z")
CTX_AXES = CHIP_AXES + ("core",)
CTX_SIZES = (4, 2, 8, 2)

f32 = jnp.float32
bf16 = jnp.bfloat16

in_vmem = pl.BlockSpec(memory_space=pltpu.VMEM)
in_hbm = pl.BlockSpec(memory_space=pltpu.HBM)


def call(body, out_shape, *args, scratch=(), in_specs=None, out_specs=None):
    return pl.pallas_call(
        body,
        out_shape=out_shape,
        in_specs=in_specs or [in_vmem] * len(args),
        out_specs=out_specs or jax.tree.map(lambda _: in_vmem, out_shape),
        scratch_shapes=list(scratch),
        compiler_params=pltpu.CompilerParams(vmem_limit_bytes=20 * 1024 * 1024),
    )(*args)


def shaped(*extent, dtype=f32):
    return jax.ShapeDtypeStruct(extent, dtype)


def dense_rows(group, first, tokens):
    return pl.ds(((group // SUB) * tokens + first) * SUB + group % SUB, SUB, stride=SUB)


def each_tile(first_tile, tiles, groups, body):
    def rows(tile, nothing):
        first = pl.multiple_of(tile * ROWS16, ROWS16)
        for group in range(groups):
            body(first, group)
        return nothing

    lax.fori_loop(first_tile, first_tile + tiles, rows, 0)


def load_dense(ref, group, first, tokens):
    return jnp.concatenate(
        [ref[dense_rows(group, first + shift, tokens), :] for shift in (0, SUB)], axis=0
    )


def store_dense(ref, group, first, tokens, value):
    for shift in (0, SUB):
        ref[dense_rows(group, first + shift, tokens), :] = value[shift : shift + SUB]


def lanes_of(group):
    return pl.ds(group * LANES, LANES)


def tile_of(ref, first, group):
    return ref[pl.ds(first, ROWS16), lanes_of(group)].astype(f32)


def half_rows(block, mode, groups):
    return pl.ds(mode * groups + block * SUB, SUB)


def half_of(ref, block, groups):
    return [ref[half_rows(block, mode, groups), :] for mode in range(HALF_MODES)]


def core_half(ref, block, groups, mine):
    core = lax.axis_index("core")
    first = (core if mine else 1 - core) * (HALF_MODES * groups)
    return [
        ref[pl.ds(pl.multiple_of(first + mode * groups + block * SUB, SUB), SUB), :]
        for mode in range(HALF_MODES)
    ]


def both_halves(ref, block, groups):
    return core_half(ref, block, groups, True) + core_half(ref, block, groups, False)


def my_rows(half):
    return pl.ds(pl.multiple_of(lax.axis_index("core") * half, half), half)


def tree_sum(terms):
    while len(terms) > 1:
        pairs = [a + b for a, b in zip(terms[::2], terms[1::2])]
        terms = pairs + terms[len(pairs) * 2 :]
    return terms[0]


def over_tokens(first, count, step, carried, backward=False):
    def several(turn, carried):
        for inner in range(UNROLL):
            at = turn * UNROLL + inner
            carried = step(first + (count - 1 - at if backward else at), carried)
        return carried

    return lax.fori_loop(0, count // UNROLL, several, carried)


def token_row(block, token, tokens):
    return pl.ds(pl.multiple_of((block * tokens + token) * SUB, SUB), SUB)


def zero_states(count):
    return [jnp.zeros((SUB, LANES), f32)] * count


def local_ends(tokens, groups, key, value, decay, residue, gain, product, keep, send, shrink, whole, weight, scale_dense, gain_in,
               key_in, value_in, rate_in, residue_in, whole_all, arrived):
    whole_copies = [
        pltpu.make_async_copy(source, target, arrived.at[2 * CHUNKS + which])
        for which, (source, target) in enumerate(((decay, rate_in), (residue, residue_in), (gain, gain_in)))
    ]
    for copy in whole_copies[:2]:
        copy.start()
    some = tokens // CHUNKS
    copies = []
    for chunk in range(CHUNKS):
        rows = pl.ds(chunk * some, some)
        pair = [
            pltpu.make_async_copy(source.at[rows, :], target.at[rows, :], arrived.at[2 * chunk + which])
            for which, (source, target) in enumerate(((key, key_in), (value, value_in)))
        ]
        for copy in pair:
            copy.start()
        copies.append(pair)
    whole_copies[2].start()
    for copy in whole_copies[:2]:
        copy.wait()
    for group in range(groups):
        rows = pl.ds(group, MODES, stride=groups)
        rate = rate_in[:, lanes_of(group)]
        in_scale = jnp.sqrt(one_minus_exp_of_minus(2.0 * rate))
        shrink[rows, :] = jnp.exp(-rate)
        whole_all[rows, :] = jnp.exp(-rate * tokens)
        scale_dense[rows, :] = in_scale
        weight[rows, :] = in_scale * residue_in[:, lanes_of(group)]
    whole[...] = whole_all[my_rows(HALF_MODES * groups), :]

    def multiply(first, group):
        store_dense(product, group, first, tokens, tile_of(key_in, first, group) * tile_of(value_in, first, group))

    for chunk in range(CHUNKS):
        for copy in copies[chunk]:
            copy.wait()
        tiles = some // ROWS16
        each_tile(chunk * tiles, tiles, groups, multiply)
        for block in range(groups // SUB):
            ratio = both_halves(shrink, block, groups)

            def step(token, states):
                row = product[token_row(block, token, tokens), :]
                return [r * s + row for r, s in zip(ratio, states)]

            states = half_of(keep, block, groups) + half_of(send, block, groups) if chunk else zero_states(MODES)
            states = over_tokens(chunk * some, some, step, states)
            for mode in range(HALF_MODES):
                keep[half_rows(block, mode, groups), :] = states[mode]
                send[half_rows(block, mode, groups), :] = states[HALF_MODES + mode]
    whole_copies[2].wait()


def one_minus_exp_of_minus(value):
    series = 1.0 - value / 9.0
    for divisor in range(8, 1, -1):
        series = 1.0 - value / divisor * series
    return jnp.where(value < 0.25, value * series, 1.0 - jnp.exp(-value))


def prepare(tokens, groups, query, grad, gain, asked, squared):
    def multiply(first, group):
        rows = tile_of(query, first, group)
        store_dense(asked, group, first, tokens, gain[:, lanes_of(group)] * tile_of(grad, first, group) * rows)
        store_dense(squared, group, first, tokens, rows * rows)

    each_tile(0, tokens // ROWS16, groups, multiply)


def chip_total(whole, keep, recv, total):
    mine_is_farther = lax.axis_index("core") == 0
    mine, other = keep[...], recv[...]
    farther = jnp.where(mine_is_farther, mine, other)
    nearer = jnp.where(mine_is_farther, other, mine)
    total[...] = whole[...] * farther + nearer


def chip_scan(chips, whole_cut, totals, before):
    ratio = whole_cut[lax.axis_index(CHIP_AXES)]
    ratio = ratio * ratio

    def step(at, state):
        before[at] = state
        return ratio * state + totals[at]

    lax.fori_loop(0, chips, step, jnp.zeros_like(ratio), unroll=8)


def core_states(whole, chip_state, keep, recv, mine, other):
    mine_is_farther = lax.axis_index("core") == 0
    farther = jnp.where(mine_is_farther, keep[...], recv[...])
    first = chip_state[...]
    second = whole[...] * first + farther
    mine[...] = jnp.where(mine_is_farther, first, second)
    other[...] = jnp.where(mine_is_farther, second, first)


def filter_mine(tokens, groups, product, shrink, weight, entry, partial):
    for pair in range(0, groups // SUB, 2):
        blocks = (pair, pair + 1)
        ratio = [core_half(shrink, block, groups, True) for block in blocks]
        factor = [core_half(weight, block, groups, True) for block in blocks]

        def step(token, states):
            result = []
            for which, block in enumerate(blocks):
                at = token_row(block, token, tokens)
                row = product[at, :]
                now = [r * s + row for r, s in zip(ratio[which], states[which])]
                partial[at, :] = tree_sum([w * s for w, s in zip(factor[which], now)])
                result.append(now)
            return result

        over_tokens(0, tokens, step, [half_of(entry, block, groups) for block in blocks])


def filter_other(tokens, groups, product, shrink, weight, entry, partial, asked, squared, filtered, curved, sums, squares, dots):
    for pair in range(0, groups // SUB, 2):
        blocks = (pair, pair + 1)
        ratio = [core_half(shrink, block, groups, False) for block in blocks]
        factor = [core_half(weight, block, groups, False) for block in blocks]

        def step(token, states):
            result, square_terms, dot_terms = [], [], []
            for which, block in enumerate(blocks):
                at = token_row(block, token, tokens)
                row = product[at, :]
                now = [r * s + row for r, s in zip(ratio[which], states[which])]
                value = partial[at, :] + tree_sum([w * s for w, s in zip(factor[which], now)])
                bent = squared[at, :] * value
                filtered[at, :] = value
                curved[at, :] = bent
                square_terms.append(bent * value)
                dot_terms.append(asked[at, :] * value)
                result.append(now)
            rows = token_row(0, token, tokens)
            if pair:
                square_terms.append(squares[rows, :])
                dot_terms.append(dots[rows, :])
            squares[rows, :] = tree_sum(square_terms)
            dots[rows, :] = tree_sum(dot_terms)
            return result

        over_tokens(0, tokens, step, [half_of(entry, block, groups) for block in blocks])
    for line, ref in enumerate((squares, dots)):
        per_token = tree_sum([ref[pl.ds(shift, tokens, stride=SUB), :] for shift in range(SUB)])
        sums[line : line + 1, :] = jnp.sum(per_token.T, axis=0, keepdims=True)


def local_adjoint(tokens, groups, sums, other_sums, asked, curved, product, shrink, scale_dense, entry_mine, entry_other,
                  inverse, slope, grad_filtered, keep, send):
    both = sums[...] + other_sums[...]
    rms = jnp.sqrt(both[0:1] / D + norm_eps)
    inverse[...] = jnp.broadcast_to(1.0 / rms, (LANES, tokens)).T
    slope[...] = jnp.broadcast_to(both[1:2] / (D * rms * rms * rms), (LANES, tokens)).T
    for block in range(groups // SUB):
        ratio = both_halves(shrink, block, groups)

        def step(token, carried):
            states, terms = carried
            at = token_row(block, token, tokens)
            now = pl.ds(token, 1)
            row = inverse[now, :] * asked[at, :] - slope[now, :] * curved[at, :]
            grad_filtered[at, :] = row
            put_in = product[at, :]
            states = [r * s + row for r, s in zip(ratio, states)]
            terms = [q + put_in * s for q, s in zip(terms, states)]
            return states, terms

        states, terms = over_tokens(0, tokens, step, (zero_states(MODES), zero_states(MODES)), backward=True)
        entry = half_of(entry_mine, block, groups) + half_of(entry_other, block, groups)
        scale = both_halves(scale_dense, block, groups)
        terms = [i * (q + r * s * e) for i, q, r, s, e in zip(scale, terms, ratio, states, entry)]
        for mode in range(HALF_MODES):
            rows = half_rows(block, mode, groups)
            keep[0, rows, :], keep[1, rows, :] = states[mode], terms[mode]
            send[0, rows, :], send[1, rows, :] = states[HALF_MODES + mode], terms[HALF_MODES + mode]


def tile_copies(tile, sent, *pairs):
    rows = pl.ds(pl.multiple_of(tile * ROWS16, ROWS16), ROWS16)
    return [
        pltpu.make_async_copy(source.at[rows, :], target.at[rows, :], sent.at[which, tile])
        for which, (source, target) in enumerate(pairs)
    ]


def norm_rows(tokens, groups, inverse, slope, filtered, query, grad, gain, normed, grad_query, normed_out, grad_out, sent):
    pairs = ((normed_out, normed), (grad_out, grad_query))
    tiles = tokens // ROWS16

    def chunk(tile, nothing):
        first = pl.multiple_of(tile * ROWS16, ROWS16)
        rows = pl.ds(first, ROWS16)
        for group in range(groups):
            part = load_dense(filtered, group, first, tokens)
            gated = tile_of(query, first, group) * part
            gains = gain[:, lanes_of(group)]
            scale = inverse[rows, :]
            normed_out[rows, lanes_of(group)] = (gated * gains * scale).astype(bf16)
            grad_gated = gains * tile_of(grad, first, group) * scale - gated * slope[rows, :]
            grad_out[rows, lanes_of(group)] = (grad_gated * part).astype(bf16)
        for copy in tile_copies(tile, sent, *pairs):
            copy.start()
        return nothing

    lax.fori_loop(0, tiles, chunk, 0)
    for tile in range(tiles):
        for copy in tile_copies(tile, sent, *pairs):
            copy.wait()


def chip_total_and_sum(half, chips, whole, keep, recv, total):
    core = lax.axis_index("core")
    mine, other = keep[0], recv[0]
    farther = jnp.where(core == 1, mine, other)
    nearer = jnp.where(core == 1, other, mine)
    cut = half // chips
    total[:, 0] = (whole[...] * farther + nearer).reshape(chips, cut, LANES)
    total[:, 1] = (keep[1] + recv[1]).reshape(chips, cut, LANES)


def chip_scan_and_sum(chips, whole_cut, totals, before):
    ratio = whole_cut[lax.axis_index(CHIP_AXES)]
    ratio = ratio * ratio

    def step(turn, carried):
        state, total = carried
        at = chips - 1 - turn
        before[at, 0] = state
        return ratio * state + totals[at, 0], total + totals[at, 1]

    zero = jnp.zeros_like(ratio)
    _, total = lax.fori_loop(0, chips, step, (zero, zero), unroll=8)
    before[:, 1] = jnp.broadcast_to(total[None], before[:, 1].shape)


def core_states_and_sum(half, whole, chip_state, keep, recv, mine, other):
    core = lax.axis_index("core")
    farther = jnp.where(core == 1, keep[0], recv[0])
    first = chip_state[:, 0].reshape(half, LANES)
    second = whole[...] * first + farther
    mine[0] = jnp.where(core == 1, first, second)
    other[0] = jnp.where(core == 1, second, first)
    summed = chip_state[:, 1].reshape(half, LANES)
    mine[1] = summed
    other[1] = summed


def grad_mine(tokens, groups, grad_filtered, shrink, weight, after, partial):
    for pair in range(0, groups // SUB, 2):
        blocks = (pair, pair + 1)
        ratio = [core_half(shrink, block, groups, True) for block in blocks]
        factor = [core_half(weight, block, groups, True) for block in blocks]

        def step(token, states):
            result = []
            for which, block in enumerate(blocks):
                at = token_row(block, token, tokens)
                row = grad_filtered[at, :]
                now = [r * s + row for r, s in zip(ratio[which], states[which])]
                partial[at, :] = tree_sum([w * s for w, s in zip(factor[which], now)])
                result.append(now)
            return result

        over_tokens(0, tokens, step, [half_of(after.at[0], block, groups) for block in blocks], backward=True)


def grad_rows(tokens, groups, grad_filtered, shrink, weight, after_mine, after_other, partial, key, value,
              grad_key, grad_value, grad_residue, total, dense, key_out, value_out, residue_out, sent, residue_sent):
    half = HALF_MODES * groups
    core = lax.axis_index("core")
    total[my_rows(half), :] = after_mine[1]
    total[pl.ds(pl.multiple_of((1 - core) * half, half), half), :] = after_other[1]
    for group in range(groups):
        residue_out[:, lanes_of(group)] = total[pl.ds(group, MODES, stride=groups), :]
    residue_copy = pltpu.make_async_copy(residue_out, grad_residue, residue_sent)
    residue_copy.start()
    blocks = groups // SUB
    tiles = tokens // ROWS16

    pairs = ((key_out, grad_key), (value_out, grad_value))

    def chunk(turn, states):
        tile = tiles - 1 - turn
        first = pl.multiple_of(tile * ROWS16, ROWS16)
        rows = pl.ds(first, ROWS16)
        states = [list(part) for part in states]
        for block in range(blocks):
            ratio = core_half(shrink, block, groups, False)
            factor = core_half(weight, block, groups, False)
            for inner in range(ROWS16 - 1, -1, -1):
                at = token_row(block, first + inner, tokens)
                row = grad_filtered[at, :]
                states[block] = [r * s + row for r, s in zip(ratio, states[block])]
                part = partial[at, :] + tree_sum([w * s for w, s in zip(factor, states[block])])
                dense[block, inner * SUB : (inner + 1) * SUB, :] = part
            for group in range(block * SUB, (block + 1) * SUB):
                part = dense[block, pl.ds(group % SUB, ROWS16, stride=SUB), :]
                key_out[rows, lanes_of(group)] = (part * tile_of(value, first, group)).astype(bf16)
                value_out[rows, lanes_of(group)] = (part * tile_of(key, first, group)).astype(bf16)
        for copy in tile_copies(tile, sent, *pairs):
            copy.start()
        return states

    lax.fori_loop(0, tiles, chunk, [half_of(after_other.at[0], block, groups) for block in range(blocks)])
    for tile in range(tiles):
        for copy in tile_copies(tile, sent, *pairs):
            copy.wait()
    residue_copy.wait()


def swap(value, axis):
    return lax.ppermute(value, axis, [(0, 1), (1, 0)])


def on_device(query_rows, key_rows, value_rows, decay_rate, residue, norm_gain, grad_out):
    tokens, channels = query_rows.shape
    groups = channels // LANES
    half = HALF_MODES * groups
    chips = lax.axis_size(CHIP_AXES)
    cut = half // chips
    natural = shaped(tokens, channels, dtype=bf16)
    dense = shaped(tokens * groups + SUB, LANES)
    modal = shaped(2 * half + groups, LANES)
    halved = shaped(half, LANES)
    two_halves = shaped(2, half, LANES)
    square = shaped(tokens, LANES)
    modal_scratch = pltpu.VMEM((2 * half + groups, LANES), f32)
    natural_scratch = pltpu.VMEM((tokens, channels), bf16)
    token_scratch = pltpu.VMEM((tokens * SUB + SUB, LANES), f32)
    bind = functools.partial

    product, keep, send, shrink, whole, weight, scale_dense, gain = call(
        bind(local_ends, tokens, groups),
        (dense, halved, halved, modal, halved, modal, modal, shaped(1, channels)),
        *[pltpu.with_memory_space_constraint(a, pltpu.HBM) for a in (key_rows, value_rows, decay_rate, residue, norm_gain[None, :])],
        in_specs=[in_hbm] * 5,
        scratch=[
            natural_scratch, natural_scratch, *[pltpu.VMEM((MODES, channels), f32)] * 2, modal_scratch,
            pltpu.SemaphoreType.DMA((2 * CHUNKS + 3,)),
        ],
    )
    whole_cut = whole.reshape(chips, cut, LANES)
    recv = swap(send, "core")
    asked, squared = call(bind(prepare, tokens, groups), (dense, dense), query_rows, grad_out, gain)
    recv, asked, squared = lax.optimization_barrier((recv, asked, squared))
    total = call(chip_total, halved, whole, keep, recv)
    totals = lax.all_to_all(total.reshape(chips, cut, LANES), CHIP_AXES, 0, 0)
    before = call(bind(chip_scan, chips), shaped(chips, cut, LANES), whole_cut, totals)
    chip_state = lax.all_to_all(before, CHIP_AXES, 0, 0).reshape(half, LANES)
    entry_mine, entry_send = call(core_states, (halved, halved), whole, chip_state, keep, recv)
    entry_other = swap(entry_send, "core")

    partial = call(bind(filter_mine, tokens, groups), dense, product, shrink, weight, entry_mine)
    filtered, curved, sums = call(
        bind(filter_other, tokens, groups),
        (dense, dense, shaped(2, tokens)),
        product, shrink, weight, entry_other, partial, asked, squared,
        scratch=[token_scratch, token_scratch],
    )
    other_sums = swap(sums, "tp")

    inverse, slope, grad_filtered, keep, send = call(
        bind(local_adjoint, tokens, groups),
        (square, square, dense, two_halves, two_halves),
        sums, other_sums, asked, curved, product, shrink, scale_dense, entry_mine, entry_other,
    )
    recv = swap(send, "core")
    normed_out, grad_query = call(
        bind(norm_rows, tokens, groups), (natural, natural), inverse, slope, filtered, query_rows, grad_out, gain,
        out_specs=(in_hbm, in_hbm),
        scratch=[natural_scratch, natural_scratch, pltpu.SemaphoreType.DMA((2, tokens // ROWS16))],
    )
    recv, normed_out, grad_query = lax.optimization_barrier((recv, normed_out, grad_query))
    total = call(bind(chip_total_and_sum, half, chips), shaped(chips, 2, cut, LANES), whole, keep, recv)
    totals = lax.all_to_all(total, CHIP_AXES, 0, 0)
    before = call(bind(chip_scan_and_sum, chips), shaped(chips, 2, cut, LANES), whole_cut, totals)
    chip_state = lax.all_to_all(before, CHIP_AXES, 0, 0)
    after_mine, after_send = call(
        bind(core_states_and_sum, half), (two_halves, two_halves), whole, chip_state, keep, recv
    )
    after_other = swap(after_send, "core")

    partial = call(bind(grad_mine, tokens, groups), dense, grad_filtered, shrink, weight, after_mine)
    grad_key, grad_value, grad_residue = call(
        bind(grad_rows, tokens, groups),
        (natural, natural, shaped(MODES, channels)),
        grad_filtered, shrink, weight, after_mine, after_other, partial, key_rows, value_rows,
        out_specs=(in_hbm, in_hbm, in_hbm),
        scratch=[
            modal_scratch, pltpu.VMEM((groups // SUB, ROWS16 * SUB + SUB, LANES), f32), natural_scratch, natural_scratch,
            pltpu.VMEM((MODES, channels), f32), pltpu.SemaphoreType.DMA((2, tokens // ROWS16)), pltpu.SemaphoreType.DMA,
        ],
    )
    return (normed_out, grad_query, grad_key, grad_value, grad_residue)


def solution(mesh):
    devices = mesh.devices
    cut_mesh = Mesh(devices.reshape(CTX_SIZES + (devices.shape[1],)), CTX_AXES + ("tp",))
    token_split = P(CTX_AXES, "tp")
    return jax.shard_map(
        on_device,
        mesh=cut_mesh,
        in_specs=(token_split, token_split, token_split, P(None, "tp"), P(None, "tp"), P("tp"), token_split),
        out_specs=(token_split, token_split, token_split, token_split, P(None, "tp")),
        check_vma=False,
    )
```

```python
import functools

import jax
import jax.numpy as jnp
from jax import lax
from jax.experimental import pallas as pl
from jax.experimental.pallas import tpu as pltpu
from jax.sharding import Mesh, PartitionSpec as P

D = 8192
MODES = 8
HALF_MODES = MODES // 2
norm_eps = 1e-05

LANES = 128
SUB = 8
ROWS16 = 16
UNROLL = 8
CHUNKS = ((0, 2), (2, 8))

CHIP_AXES = ("x", "yl", "z")
CTX_AXES = CHIP_AXES + ("core",)
CTX_SIZES = (4, 2, 8, 2)

f32 = jnp.float32
bf16 = jnp.bfloat16

in_vmem = pl.BlockSpec(memory_space=pltpu.VMEM)
in_hbm = pl.BlockSpec(memory_space=pltpu.HBM)


def call(body, out_shape, *args, scratch=(), in_specs=None, out_specs=None):
    return pl.pallas_call(
        body,
        out_shape=out_shape,
        in_specs=in_specs or [in_vmem] * len(args),
        out_specs=out_specs or jax.tree.map(lambda _: in_vmem, out_shape),
        scratch_shapes=list(scratch),
        compiler_params=pltpu.CompilerParams(vmem_limit_bytes=20 * 1024 * 1024),
    )(*args)


def shaped(*extent, dtype=f32):
    return jax.ShapeDtypeStruct(extent, dtype)


def dense_rows(group, first, tokens):
    return pl.ds(((group // SUB) * tokens + first) * SUB + group % SUB, SUB, stride=SUB)


def each_tile(first_tile, tiles, groups, body):
    def rows(tile, nothing):
        first = pl.multiple_of(tile * ROWS16, ROWS16)
        for group in range(groups):
            body(first, group)
        return nothing

    lax.fori_loop(first_tile, first_tile + tiles, rows, 0)


def load_dense(ref, group, first, tokens):
    return jnp.concatenate(
        [ref[dense_rows(group, first + shift, tokens), :] for shift in (0, SUB)], axis=0
    )


def store_dense(ref, group, first, tokens, value):
    for shift in (0, SUB):
        ref[dense_rows(group, first + shift, tokens), :] = value[shift : shift + SUB]


def lanes_of(group):
    return pl.ds(group * LANES, LANES)


def tile_of(ref, first, group):
    return ref[pl.ds(first, ROWS16), lanes_of(group)].astype(f32)


def half_rows(block, mode, groups):
    return pl.ds(mode * groups + block * SUB, SUB)


def half_of(ref, block, groups):
    return [ref[half_rows(block, mode, groups), :] for mode in range(HALF_MODES)]


def core_half(ref, block, groups, mine):
    core = lax.axis_index("core")
    first = (core if mine else 1 - core) * (HALF_MODES * groups)
    return [
        ref[pl.ds(pl.multiple_of(first + mode * groups + block * SUB, SUB), SUB), :]
        for mode in range(HALF_MODES)
    ]


def both_halves(ref, block, groups):
    return core_half(ref, block, groups, True) + core_half(ref, block, groups, False)


def my_rows(half):
    return pl.ds(pl.multiple_of(lax.axis_index("core") * half, half), half)


def tree_sum(terms):
    while len(terms) > 1:
        pairs = [a + b for a, b in zip(terms[::2], terms[1::2])]
        terms = pairs + terms[len(pairs) * 2 :]
    return terms[0]


def over_tokens(first, count, step, carried, backward=False):
    def several(turn, carried):
        for inner in range(UNROLL):
            at = turn * UNROLL + inner
            carried = step(first + (count - 1 - at if backward else at), carried)
        return carried

    return lax.fori_loop(0, count // UNROLL, several, carried)


def token_row(block, token, tokens):
    return pl.ds(pl.multiple_of((block * tokens + token) * SUB, SUB), SUB)


def zero_states(count):
    return [jnp.zeros((SUB, LANES), f32)] * count


def local_ends(tokens, groups, key, value, decay, residue, gain,
               product, keep, send, shrink, whole, key_in, value_in, rate_in, residue_in, gain_in, whole_all, arrived):
    rate_copy, *later_copies = [
        pltpu.make_async_copy(source, target, arrived.at[2 * len(CHUNKS) + which])
        for which, (source, target) in enumerate(((decay, rate_in), (residue, residue_in), (gain, gain_in)))
    ]
    rate_copy.start()
    copies = []
    for chunk, (begin, end) in enumerate(CHUNKS):
        rows = pl.ds(begin * tokens // 8, (end - begin) * tokens // 8)
        pair = [
            pltpu.make_async_copy(source.at[rows, :], target.at[rows, :], arrived.at[2 * chunk + which])
            for which, (source, target) in enumerate(((key, key_in), (value, value_in)))
        ]
        for copy in pair:
            copy.start()
        copies.append(pair)
    for copy in later_copies:
        copy.start()
    rate_copy.wait()
    for group in range(groups):
        rows = pl.ds(group, MODES, stride=groups)
        rate = rate_in[:, lanes_of(group)]
        shrink[rows, :] = jnp.exp(-rate)
        whole_all[rows, :] = jnp.exp(-rate * tokens)
    whole[...] = whole_all[my_rows(HALF_MODES * groups), :]

    def multiply(first, group):
        store_dense(product, group, first, tokens, tile_of(key_in, first, group) * tile_of(value_in, first, group))

    for chunk, (begin, end) in enumerate(CHUNKS):
        for copy in copies[chunk]:
            copy.wait()
        first, some = begin * tokens // 8, (end - begin) * tokens // 8
        each_tile(first // ROWS16, some // ROWS16, groups, multiply)
        for block in range(groups // SUB):
            ratio = both_halves(shrink, block, groups)

            def step(token, states):
                row = product[token_row(block, token, tokens), :]
                return [r * s + row for r, s in zip(ratio, states)]

            states = half_of(keep, block, groups) + half_of(send, block, groups) if chunk else zero_states(MODES)
            states = over_tokens(first, some, step, states)
            for mode in range(HALF_MODES):
                keep[half_rows(block, mode, groups), :] = states[mode]
                send[half_rows(block, mode, groups), :] = states[HALF_MODES + mode]
    for copy in later_copies:
        copy.wait()


def one_minus_exp_of_minus(value):
    series = 1.0 - value / 9.0
    for divisor in range(8, 1, -1):
        series = 1.0 - value / divisor * series
    return jnp.where(value < 0.25, value * series, 1.0 - jnp.exp(-value))


def prepare(tokens, groups, query, grad, gain, decay, residue, asked, squared, weight, scale_dense):
    for group in range(groups):
        rows = pl.ds(group, MODES, stride=groups)
        in_scale = jnp.sqrt(one_minus_exp_of_minus(2.0 * decay[:, lanes_of(group)]))
        scale_dense[rows, :] = in_scale
        weight[rows, :] = in_scale * residue[:, lanes_of(group)]

    def multiply(first, group):
        rows = tile_of(query, first, group)
        store_dense(asked, group, first, tokens, gain[:, lanes_of(group)] * tile_of(grad, first, group) * rows)
        store_dense(squared, group, first, tokens, rows * rows)

    each_tile(0, tokens // ROWS16, groups, multiply)


def chip_total(whole, keep, recv, total):
    mine_is_farther = lax.axis_index("core") == 0
    mine, other = keep[...], recv[...]
    farther = jnp.where(mine_is_farther, mine, other)
    nearer = jnp.where(mine_is_farther, other, mine)
    total[...] = whole[...] * farther + nearer


def chip_scan(chips, whole_cut, totals, before):
    ratio = whole_cut[lax.axis_index(CHIP_AXES)]
    ratio = ratio * ratio

    def step(at, state):
        before[at] = state
        return ratio * state + totals[at]

    lax.fori_loop(0, chips, step, jnp.zeros_like(ratio), unroll=8)


def core_states(whole, chip_state, keep, recv, mine, other):
    mine_is_farther = lax.axis_index("core") == 0
    farther = jnp.where(mine_is_farther, keep[...], recv[...])
    first = chip_state[...]
    second = whole[...] * first + farther
    mine[...] = jnp.where(mine_is_farther, first, second)
    other[...] = jnp.where(mine_is_farther, second, first)


def filter_mine(tokens, groups, product, shrink, weight, entry, partial):
    for pair in range(0, groups // SUB, 2):
        blocks = (pair, pair + 1)
        ratio = [core_half(shrink, block, groups, True) for block in blocks]
        factor = [core_half(weight, block, groups, True) for block in blocks]

        def step(token, states):
            result = []
            for which, block in enumerate(blocks):
                at = token_row(block, token, tokens)
                row = product[at, :]
                now = [r * s + row for r, s in zip(ratio[which], states[which])]
                partial[at, :] = tree_sum([w * s for w, s in zip(factor[which], now)])
                result.append(now)
            return result

        over_tokens(0, tokens, step, [half_of(entry, block, groups) for block in blocks])


def filter_other(tokens, groups, product, shrink, weight, entry, partial, asked, squared, filtered, curved, sums, squares, dots):
    for pair in range(0, groups // SUB, 2):
        blocks = (pair, pair + 1)
        ratio = [core_half(shrink, block, groups, False) for block in blocks]
        factor = [core_half(weight, block, groups, False) for block in blocks]

        def step(token, states):
            result, square_terms, dot_terms = [], [], []
            for which, block in enumerate(blocks):
                at = token_row(block, token, tokens)
                row = product[at, :]
                now = [r * s + row for r, s in zip(ratio[which], states[which])]
                value = partial[at, :] + tree_sum([w * s for w, s in zip(factor[which], now)])
                bent = squared[at, :] * value
                filtered[at, :] = value
                curved[at, :] = bent
                square_terms.append(bent * value)
                dot_terms.append(asked[at, :] * value)
                result.append(now)
            rows = token_row(0, token, tokens)
            if pair:
                square_terms.append(squares[rows, :])
                dot_terms.append(dots[rows, :])
            squares[rows, :] = tree_sum(square_terms)
            dots[rows, :] = tree_sum(dot_terms)
            return result

        over_tokens(0, tokens, step, [half_of(entry, block, groups) for block in blocks])
    for line, ref in enumerate((squares, dots)):
        per_token = tree_sum([ref[pl.ds(shift, tokens, stride=SUB), :] for shift in range(SUB)])
        sums[line : line + 1, :] = jnp.sum(per_token.T, axis=0, keepdims=True)


def local_adjoint(tokens, groups, sums, other_sums, asked, curved, product, shrink, scale_dense, entry_mine, entry_other,
                  inverse, slope, grad_filtered, keep, send):
    both = sums[...] + other_sums[...]
    rms = jnp.sqrt(both[0:1] / D + norm_eps)
    inverse[...] = jnp.broadcast_to(1.0 / rms, (LANES, tokens)).T
    slope[...] = jnp.broadcast_to(both[1:2] / (D * rms * rms * rms), (LANES, tokens)).T
    for block in range(groups // SUB):
        ratio = both_halves(shrink, block, groups)

        def step(token, carried):
            states, terms = carried
            at = token_row(block, token, tokens)
            now = pl.ds(token, 1)
            row = inverse[now, :] * asked[at, :] - slope[now, :] * curved[at, :]
            grad_filtered[at, :] = row
            put_in = product[at, :]
            states = [r * s + row for r, s in zip(ratio, states)]
            terms = [q + put_in * s for q, s in zip(terms, states)]
            return states, terms

        states, terms = over_tokens(0, tokens, step, (zero_states(MODES), zero_states(MODES)), backward=True)
        entry = half_of(entry_mine, block, groups) + half_of(entry_other, block, groups)
        scale = both_halves(scale_dense, block, groups)
        terms = [i * (q + r * s * e) for i, q, r, s, e in zip(scale, terms, ratio, states, entry)]
        for mode in range(HALF_MODES):
            rows = half_rows(block, mode, groups)
            keep[0, rows, :], keep[1, rows, :] = states[mode], terms[mode]
            send[0, rows, :], send[1, rows, :] = states[HALF_MODES + mode], terms[HALF_MODES + mode]


def tile_copies(tile, sent, *pairs):
    rows = pl.ds(pl.multiple_of(tile * ROWS16, ROWS16), ROWS16)
    return [
        pltpu.make_async_copy(source.at[rows, :], target.at[rows, :], sent.at[which, tile])
        for which, (source, target) in enumerate(pairs)
    ]


def norm_rows(tokens, groups, inverse, slope, filtered, query, grad, gain, normed, grad_query):
    def finish(first, group):
        rows = pl.ds(first, ROWS16)
        part = load_dense(filtered, group, first, tokens)
        gated = tile_of(query, first, group) * part
        gains = gain[:, lanes_of(group)]
        scale = inverse[rows, :]
        normed[rows, lanes_of(group)] = (gated * gains * scale).astype(bf16)
        grad_gated = gains * tile_of(grad, first, group) * scale - gated * slope[rows, :]
        grad_query[rows, lanes_of(group)] = (grad_gated * part).astype(bf16)

    each_tile(0, tokens // ROWS16, groups, finish)


def chip_total_and_sum(half, chips, whole, keep, recv, total):
    core = lax.axis_index("core")
    mine, other = keep[0], recv[0]
    farther = jnp.where(core == 1, mine, other)
    nearer = jnp.where(core == 1, other, mine)
    cut = half // chips
    total[:, 0] = (whole[...] * farther + nearer).reshape(chips, cut, LANES)
    total[:, 1] = (keep[1] + recv[1]).reshape(chips, cut, LANES)


def chip_scan_and_sum(chips, whole_cut, totals, before):
    ratio = whole_cut[lax.axis_index(CHIP_AXES)]
    ratio = ratio * ratio

    def step(turn, carried):
        state, total = carried
        at = chips - 1 - turn
        before[at, 0] = state
        return ratio * state + totals[at, 0], total + totals[at, 1]

    zero = jnp.zeros_like(ratio)
    _, total = lax.fori_loop(0, chips, step, (zero, zero), unroll=8)
    before[:, 1] = jnp.broadcast_to(total[None], before[:, 1].shape)


def core_states_and_sum(half, whole, chip_state, keep, recv, mine, other):
    core = lax.axis_index("core")
    farther = jnp.where(core == 1, keep[0], recv[0])
    first = chip_state[:, 0].reshape(half, LANES)
    second = whole[...] * first + farther
    mine[0] = jnp.where(core == 1, first, second)
    other[0] = jnp.where(core == 1, second, first)
    summed = chip_state[:, 1].reshape(half, LANES)
    mine[1] = summed
    other[1] = summed


def grad_mine(tokens, groups, grad_filtered, shrink, weight, after, partial):
    for pair in range(0, groups // SUB, 2):
        blocks = (pair, pair + 1)
        ratio = [core_half(shrink, block, groups, True) for block in blocks]
        factor = [core_half(weight, block, groups, True) for block in blocks]

        def step(token, states):
            result = []
            for which, block in enumerate(blocks):
                at = token_row(block, token, tokens)
                row = grad_filtered[at, :]
                now = [r * s + row for r, s in zip(ratio[which], states[which])]
                partial[at, :] = tree_sum([w * s for w, s in zip(factor[which], now)])
                result.append(now)
            return result

        over_tokens(0, tokens, step, [half_of(after.at[0], block, groups) for block in blocks], backward=True)


def grad_rows(tokens, groups, grad_filtered, shrink, weight, after_mine, after_other, partial, key, value, normed, grad_query,
              grad_key, grad_value, grad_residue, normed_out, grad_query_out,
              total, dense, key_out, value_out, residue_out, sent, whole_sent):
    half = HALF_MODES * groups
    core = lax.axis_index("core")
    total[my_rows(half), :] = after_mine[1]
    total[pl.ds(pl.multiple_of((1 - core) * half, half), half), :] = after_other[1]
    for group in range(groups):
        residue_out[:, lanes_of(group)] = total[pl.ds(group, MODES, stride=groups), :]
    whole_copies = [
        pltpu.make_async_copy(source, target, whole_sent.at[which])
        for which, (source, target) in enumerate(
            ((normed, normed_out), (grad_query, grad_query_out), (residue_out, grad_residue))
        )
    ]
    for copy in whole_copies:
        copy.start()
    blocks = groups // SUB
    tiles = tokens // ROWS16

    pairs = ((key_out, grad_key), (value_out, grad_value))

    def chunk(turn, states):
        tile = tiles - 1 - turn
        first = pl.multiple_of(tile * ROWS16, ROWS16)
        rows = pl.ds(first, ROWS16)
        states = [list(part) for part in states]
        for block in range(blocks):
            ratio = core_half(shrink, block, groups, False)
            factor = core_half(weight, block, groups, False)
            for inner in range(ROWS16 - 1, -1, -1):
                at = token_row(block, first + inner, tokens)
                row = grad_filtered[at, :]
                states[block] = [r * s + row for r, s in zip(ratio, states[block])]
                part = partial[at, :] + tree_sum([w * s for w, s in zip(factor, states[block])])
                dense[block, inner * SUB : (inner + 1) * SUB, :] = part
            for group in range(block * SUB, (block + 1) * SUB):
                part = dense[block, pl.ds(group % SUB, ROWS16, stride=SUB), :]
                key_out[rows, lanes_of(group)] = (part * tile_of(value, first, group)).astype(bf16)
                value_out[rows, lanes_of(group)] = (part * tile_of(key, first, group)).astype(bf16)
        for copy in tile_copies(tile, sent, *pairs):
            copy.start()
        return states

    lax.fori_loop(0, tiles, chunk, [half_of(after_other.at[0], block, groups) for block in range(blocks)])
    for tile in range(tiles):
        for copy in tile_copies(tile, sent, *pairs):
            copy.wait()
    for copy in whole_copies:
        copy.wait()


def swap(value, axis):
    return lax.ppermute(value, axis, [(0, 1), (1, 0)])


def on_device(query_rows, key_rows, value_rows, decay_rate, residue, norm_gain, grad_out):
    tokens, channels = query_rows.shape
    groups = channels // LANES
    half = HALF_MODES * groups
    chips = lax.axis_size(CHIP_AXES)
    cut = half // chips
    natural = shaped(tokens, channels, dtype=bf16)
    rates = shaped(MODES, channels)
    dense = shaped(tokens * groups + SUB, LANES)
    modal = shaped(2 * half + groups, LANES)
    halved = shaped(half, LANES)
    two_halves = shaped(2, half, LANES)
    square = shaped(tokens, LANES)
    modal_scratch = pltpu.VMEM((2 * half + groups, LANES), f32)
    natural_scratch = pltpu.VMEM((tokens, channels), bf16)
    token_scratch = pltpu.VMEM((tokens * SUB + SUB, LANES), f32)
    bind = functools.partial

    inputs = (key_rows, value_rows, decay_rate, residue, norm_gain[None, :])
    product, keep, send, shrink, whole, key_near, value_near, rate_near, residue_near, gain = call(
        bind(local_ends, tokens, groups),
        (dense, halved, halved, modal, halved, natural, natural, rates, rates, shaped(1, channels)),
        *[pltpu.with_memory_space_constraint(array, pltpu.HBM) for array in inputs],
        in_specs=[in_hbm] * len(inputs),
        scratch=[modal_scratch, pltpu.SemaphoreType.DMA((2 * len(CHUNKS) + 3,))],
    )
    whole_cut = whole.reshape(chips, cut, LANES)
    recv = swap(send, "core")
    asked, squared, weight, scale_dense = call(
        bind(prepare, tokens, groups), (dense, dense, modal, modal), query_rows, grad_out, gain, rate_near, residue_near
    )
    recv, asked = lax.optimization_barrier((recv, asked))
    total = call(chip_total, halved, whole, keep, recv)
    totals = lax.all_to_all(total.reshape(chips, cut, LANES), CHIP_AXES, 0, 0)
    before = call(bind(chip_scan, chips), shaped(chips, cut, LANES), whole_cut, totals)
    chip_state = lax.all_to_all(before, CHIP_AXES, 0, 0).reshape(half, LANES)
    entry_mine, entry_send = call(core_states, (halved, halved), whole, chip_state, keep, recv)
    entry_other = swap(entry_send, "core")

    partial = call(bind(filter_mine, tokens, groups), dense, product, shrink, weight, entry_mine)
    filtered, curved, sums = call(
        bind(filter_other, tokens, groups),
        (dense, dense, shaped(2, tokens)),
        product, shrink, weight, entry_other, partial, asked, squared,
        scratch=[token_scratch, token_scratch],
    )
    other_sums = swap(sums, "tp")

    inverse, slope, grad_filtered, keep, send = call(
        bind(local_adjoint, tokens, groups),
        (square, square, dense, two_halves, two_halves),
        sums, other_sums, asked, curved, product, shrink, scale_dense, entry_mine, entry_other,
    )
    recv = swap(send, "core")
    normed_near, grad_query_near = call(
        bind(norm_rows, tokens, groups), (natural, natural), inverse, slope, filtered, query_rows, grad_out, gain
    )
    recv, normed_near, grad_query_near = lax.optimization_barrier((recv, normed_near, grad_query_near))
    total = call(bind(chip_total_and_sum, half, chips), shaped(chips, 2, cut, LANES), whole, keep, recv)
    totals = lax.all_to_all(total, CHIP_AXES, 0, 0)
    before = call(bind(chip_scan_and_sum, chips), shaped(chips, 2, cut, LANES), whole_cut, totals)
    chip_state = lax.all_to_all(before, CHIP_AXES, 0, 0)
    after_mine, after_send = call(
        bind(core_states_and_sum, half), (two_halves, two_halves), whole, chip_state, keep, recv
    )
    after_other = swap(after_send, "core")

    partial = call(bind(grad_mine, tokens, groups), dense, grad_filtered, shrink, weight, after_mine)
    grad_key, grad_value, grad_residue, normed_out, grad_query = call(
        bind(grad_rows, tokens, groups),
        (natural, natural, rates, natural, natural),
        grad_filtered, shrink, weight, after_mine, after_other, partial, key_near, value_near, normed_near, grad_query_near,
        out_specs=(in_hbm,) * 5,
        scratch=[
            modal_scratch, pltpu.VMEM((groups // SUB, ROWS16 * SUB + SUB, LANES), f32), natural_scratch, natural_scratch,
            pltpu.VMEM((MODES, channels), f32), pltpu.SemaphoreType.DMA((2, tokens // ROWS16)), pltpu.SemaphoreType.DMA((3,)),
        ],
    )
    return (normed_out, grad_query, grad_key, grad_value, grad_residue)


def solution(mesh):
    devices = mesh.devices
    cut_mesh = Mesh(devices.reshape(CTX_SIZES + (devices.shape[1],)), CTX_AXES + ("tp",))
    token_split = P(CTX_AXES, "tp")
    return jax.shard_map(
        on_device,
        mesh=cut_mesh,
        in_specs=(token_split, token_split, token_split, P(None, "tp"), P(None, "tp"), P("tp"), token_split),
        out_specs=(token_split, token_split, token_split, token_split, P(None, "tp")),
        check_vma=False,
    )
```

```python
import functools

import jax
import jax.numpy as jnp
from jax import lax
from jax.experimental import pallas as pl
from jax.experimental.pallas import tpu as pltpu
from jax.sharding import Mesh, PartitionSpec as P

D = 8192
MODES = 8
HALF_MODES = MODES // 2
norm_eps = 1e-05

LANES = 128
SUB = 8
ROWS16 = 16
STEP = 4
CHUNKS = ((0, 2), (2, 8))

CHIP_AXES = ("x", "yl", "z")
CTX_AXES = CHIP_AXES + ("core",)
CTX_SIZES = (4, 2, 8, 2)

f32 = jnp.float32
bf16 = jnp.bfloat16

in_vmem = pl.BlockSpec(memory_space=pltpu.VMEM)
in_hbm = pl.BlockSpec(memory_space=pltpu.HBM)


def call(body, out_shape, *args, scratch=(), in_specs=None, out_specs=None):
    return pl.pallas_call(
        body,
        out_shape=out_shape,
        in_specs=in_specs or [in_vmem] * len(args),
        out_specs=out_specs or jax.tree.map(lambda _: in_vmem, out_shape),
        scratch_shapes=list(scratch),
        compiler_params=pltpu.CompilerParams(vmem_limit_bytes=20 * 1024 * 1024),
    )(*args)


def shaped(*extent, dtype=f32):
    return jax.ShapeDtypeStruct(extent, dtype)


def dense_rows(group, first, tokens):
    return pl.ds(((group // SUB) * tokens + first) * SUB + group % SUB, SUB, stride=SUB)


def each_tile(first_tile, tiles, groups, body):
    def rows(tile, nothing):
        first = pl.multiple_of(tile * ROWS16, ROWS16)
        for group in range(groups):
            body(first, group)
        return nothing

    lax.fori_loop(first_tile, first_tile + tiles, rows, 0)


def load_dense(ref, group, first, tokens):
    return jnp.concatenate(
        [ref[dense_rows(group, first + shift, tokens), :] for shift in (0, SUB)], axis=0
    )


def store_dense(ref, group, first, tokens, value):
    for shift in (0, SUB):
        ref[dense_rows(group, first + shift, tokens), :] = value[shift : shift + SUB]


def lanes_of(group):
    return pl.ds(group * LANES, LANES)


def tile_of(ref, first, group):
    return ref[pl.ds(first, ROWS16), lanes_of(group)].astype(f32)


def half_rows(block, mode, groups):
    return pl.ds(mode * groups + block * SUB, SUB)


def half_of(ref, block, groups):
    return [ref[half_rows(block, mode, groups), :] for mode in range(HALF_MODES)]


def core_half(ref, block, groups, mine):
    core = lax.axis_index("core")
    first = (core if mine else 1 - core) * (HALF_MODES * groups)
    return [
        ref[pl.ds(pl.multiple_of(first + mode * groups + block * SUB, SUB), SUB), :]
        for mode in range(HALF_MODES)
    ]


def both_halves(ref, block, groups):
    return core_half(ref, block, groups, True) + core_half(ref, block, groups, False)


def my_rows(half):
    return pl.ds(pl.multiple_of(lax.axis_index("core") * half, half), half)


def tree_sum(terms):
    while len(terms) > 1:
        pairs = [a + b for a, b in zip(terms[::2], terms[1::2])]
        terms = pairs + terms[len(pairs) * 2 :]
    return terms[0]


def over_steps(first, count, together, body, carried, backward=False):
    def several(turn, carried):
        for inner in range(together):
            at = turn * together + inner
            carried = body(first + (count - 1 - at if backward else at), carried)
        return carried

    return lax.fori_loop(0, count // together, several, carried)


def step_rows(block, step, mode, steps):
    return pl.ds(pl.multiple_of(((block * steps + step) * MODES + mode) * SUB, SUB), SUB)


def boundary(ref, block, step, steps, mine):
    modes = range(HALF_MODES) if mine else range(HALF_MODES, MODES)
    return [ref[step_rows(block, step, mode, steps), :] for mode in modes]


def put_boundary(ref, block, step, steps, states):
    for mode in range(MODES):
        ref[step_rows(block, step, mode, steps), :] = states[mode]


def powers(ratio, factor):
    rising, passed = [factor], ratio
    for turn in range(STEP):
        rising.append([f * r for f, r in zip(rising[-1], ratio)])
        if turn:
            passed = [p * r for p, r in zip(passed, ratio)]
    return rising[1:], passed


def taps(shrink, weight, block, groups):
    ratio, now = both_halves(shrink, block, groups), both_halves(weight, block, groups)
    result = []
    for _ in range(STEP):
        result.append(tree_sum(now))
        now = [n * r for n, r in zip(now, ratio)]
    return result


def token_row(block, token, tokens):
    return pl.ds(pl.multiple_of((block * tokens + token) * SUB, SUB), SUB)


def zero_states(count):
    return [jnp.zeros((SUB, LANES), f32)] * count


def local_ends(tokens, groups, key, value, decay, residue, gain,
               product, local_states, keep, send, shrink, whole, key_in, value_in, rate_in, residue_in, gain_in, whole_all, arrived):
    rate_copy, *later_copies = [
        pltpu.make_async_copy(source, target, arrived.at[2 * len(CHUNKS) + which])
        for which, (source, target) in enumerate(((decay, rate_in), (residue, residue_in), (gain, gain_in)))
    ]
    rate_copy.start()
    copies = []
    for chunk, (begin, end) in enumerate(CHUNKS):
        rows = pl.ds(begin * tokens // 8, (end - begin) * tokens // 8)
        pair = [
            pltpu.make_async_copy(source.at[rows, :], target.at[rows, :], arrived.at[2 * chunk + which])
            for which, (source, target) in enumerate(((key, key_in), (value, value_in)))
        ]
        for copy in pair:
            copy.start()
        copies.append(pair)
    for copy in later_copies:
        copy.start()
    rate_copy.wait()
    for group in range(groups):
        rows = pl.ds(group, MODES, stride=groups)
        rate = rate_in[:, lanes_of(group)]
        shrink[rows, :] = jnp.exp(-rate)
        whole_all[rows, :] = jnp.exp(-rate * tokens)
    whole[...] = whole_all[my_rows(HALF_MODES * groups), :]

    def multiply(first, group):
        store_dense(product, group, first, tokens, tile_of(key_in, first, group) * tile_of(value_in, first, group))

    for chunk, (begin, end) in enumerate(CHUNKS):
        for copy in copies[chunk]:
            copy.wait()
        first, some = begin * tokens // 8, (end - begin) * tokens // 8
        each_tile(first // ROWS16, some // ROWS16, groups, multiply)
        for block in range(groups // SUB):
            ratio = both_halves(shrink, block, groups)

            def advance(step, states):
                put_boundary(local_states, block, step, tokens // STEP, states)
                for inner in range(STEP):
                    row = product[token_row(block, step * STEP + inner, tokens), :]
                    states = [r * s + row for r, s in zip(ratio, states)]
                return states

            states = half_of(keep, block, groups) + half_of(send, block, groups) if chunk else zero_states(MODES)
            states = over_steps(first // STEP, some // STEP, 4, advance, states)
            for mode in range(HALF_MODES):
                keep[half_rows(block, mode, groups), :] = states[mode]
                send[half_rows(block, mode, groups), :] = states[HALF_MODES + mode]
    for copy in later_copies:
        copy.wait()


def one_minus_exp_of_minus(value):
    series = 1.0 - value / 9.0
    for divisor in range(8, 1, -1):
        series = 1.0 - value / divisor * series
    return jnp.where(value < 0.25, value * series, 1.0 - jnp.exp(-value))


def prepare(tokens, groups, query, grad, gain, decay, residue, asked, squared, weight, scale_dense):
    for group in range(groups):
        rows = pl.ds(group, MODES, stride=groups)
        in_scale = jnp.sqrt(one_minus_exp_of_minus(2.0 * decay[:, lanes_of(group)]))
        scale_dense[rows, :] = in_scale
        weight[rows, :] = in_scale * residue[:, lanes_of(group)]

    def multiply(first, group):
        rows = tile_of(query, first, group)
        store_dense(asked, group, first, tokens, gain[:, lanes_of(group)] * tile_of(grad, first, group) * rows)
        store_dense(squared, group, first, tokens, rows * rows)

    each_tile(0, tokens // ROWS16, groups, multiply)


def chip_total(whole, keep, recv, total):
    mine_is_farther = lax.axis_index("core") == 0
    mine, other = keep[...], recv[...]
    farther = jnp.where(mine_is_farther, mine, other)
    nearer = jnp.where(mine_is_farther, other, mine)
    total[...] = whole[...] * farther + nearer


def chip_scan(chips, whole_cut, totals, before):
    ratio = whole_cut[lax.axis_index(CHIP_AXES)]
    ratio = ratio * ratio

    def step(at, state):
        before[at] = state
        return ratio * state + totals[at]

    lax.fori_loop(0, chips, step, jnp.zeros_like(ratio), unroll=8)


def core_states(whole, chip_state, keep, recv, mine, other):
    mine_is_farther = lax.axis_index("core") == 0
    farther = jnp.where(mine_is_farther, keep[...], recv[...])
    first = chip_state[...]
    second = whole[...] * first + farther
    mine[...] = jnp.where(mine_is_farther, first, second)
    other[...] = jnp.where(mine_is_farther, second, first)


def filter_mine(tokens, groups, product, local_states, shrink, weight, entry, partial):
    steps = tokens // STEP
    for block in range(groups // SUB):
        rising, passed = powers(core_half(shrink, block, groups, True), core_half(weight, block, groups, True))
        tap = taps(shrink, weight, block, groups)

        def advance(step, entering):
            states = [s + e for s, e in zip(boundary(local_states, block, step, steps, True), entering)]
            rows = []
            for inner in range(STEP):
                at = token_row(block, step * STEP + inner, tokens)
                rows.append(product[at, :])
                own = [tap[inner - back] * rows[back] for back in range(inner + 1)]
                partial[at, :] = tree_sum([w * s for w, s in zip(rising[inner], states)] + own)
            return [p * e for p, e in zip(passed, entering)]

        over_steps(0, steps, 4, advance, half_of(entry, block, groups))


def filter_other(tokens, groups, local_states, shrink, weight, entry, partial, asked, squared, filtered, curved, sums, squares, dots):
    steps = tokens // STEP
    for block in range(groups // SUB):
        rising, passed = powers(core_half(shrink, block, groups, False), core_half(weight, block, groups, False))

        def advance(step, entering):
            states = [s + e for s, e in zip(boundary(local_states, block, step, steps, False), entering)]
            for inner in range(STEP):
                token = step * STEP + inner
                at = token_row(block, token, tokens)
                value = tree_sum([w * s for w, s in zip(rising[inner], states)]) + partial[at, :]
                bent = squared[at, :] * value
                filtered[at, :] = value
                curved[at, :] = bent
                rows = token_row(0, token, tokens)
                square_term, dot_term = bent * value, asked[at, :] * value
                squares[rows, :] = square_term + squares[rows, :] if block else square_term
                dots[rows, :] = dot_term + dots[rows, :] if block else dot_term
            return [p * e for p, e in zip(passed, entering)]

        over_steps(0, steps, 4, advance, half_of(entry, block, groups))
    for line, ref in enumerate((squares, dots)):
        per_token = tree_sum([ref[pl.ds(shift, tokens, stride=SUB), :] for shift in range(SUB)])
        sums[line : line + 1, :] = jnp.sum(per_token.T, axis=0, keepdims=True)


def step_sums(tokens, groups, product, shrink, sums):
    steps = tokens // STEP
    for block in range(groups // SUB):
        ratio = both_halves(shrink, block, groups)

        def gather(step, nothing):
            rows = [product[token_row(block, step * STEP + inner, tokens), :] for inner in range(STEP)]
            total = [r * rows[0] for r in ratio]
            for row in rows[1:]:
                total = [r * (row + t) for r, t in zip(ratio, total)]
            put_boundary(sums, block, step, steps, total)
            return nothing

        over_steps(0, steps, 4, gather, 0)


def local_adjoint(tokens, groups, sums, other_sums, asked, curved, product, product_sums, shrink, scale_dense, entry_mine, entry_other,
                  inverse, slope, grad_filtered, local_adjoints, keep, send):
    steps = tokens // STEP
    both = sums[...] + other_sums[...]
    rms = jnp.sqrt(both[0:1] / D + norm_eps)
    inverse[...] = jnp.broadcast_to(1.0 / rms, (LANES, tokens)).T
    slope[...] = jnp.broadcast_to(both[1:2] / (D * rms * rms * rms), (LANES, tokens)).T
    for block in range(groups // SUB):
        ratio = both_halves(shrink, block, groups)

        def advance(step, carried):
            states, terms, shared = carried
            put_boundary(local_adjoints, block, step, steps, states)
            along = boundary(product_sums, block, step, steps, True) + boundary(product_sums, block, step, steps, False)
            terms = [q + a * s for q, a, s in zip(terms, along, states)]
            grads = [None] * STEP
            for inner in range(STEP - 1, -1, -1):
                token = step * STEP + inner
                at = token_row(block, token, tokens)
                now = pl.ds(token, 1)
                grads[inner] = inverse[now, :] * asked[at, :] - slope[now, :] * curved[at, :]
                grad_filtered[at, :] = grads[inner]
                states = [r * s + grads[inner] for r, s in zip(ratio, states)]
                put_in = product[at, :]
                shared = [
                    c + put_in * grads[inner + apart] if inner + apart < STEP else c for apart, c in enumerate(shared)
                ]
            return states, terms, shared

        start = (zero_states(MODES), zero_states(MODES), zero_states(STEP))
        states, terms, shared = over_steps(0, steps, 2, advance, start, backward=True)
        for mode in range(MODES):
            near = shared[STEP - 1]
            for part in shared[STEP - 2 :: -1]:
                near = part + ratio[mode] * near
            terms[mode] = terms[mode] + near
        entry = half_of(entry_mine, block, groups) + half_of(entry_other, block, groups)
        scale = both_halves(scale_dense, block, groups)
        terms = [i * (q + r * s * e) for i, q, r, s, e in zip(scale, terms, ratio, states, entry)]
        for mode in range(HALF_MODES):
            rows = half_rows(block, mode, groups)
            keep[0, rows, :], keep[1, rows, :] = states[mode], terms[mode]
            send[0, rows, :], send[1, rows, :] = states[HALF_MODES + mode], terms[HALF_MODES + mode]


def tile_copies(tile, sent, *pairs):
    rows = pl.ds(pl.multiple_of(tile * ROWS16, ROWS16), ROWS16)
    return [
        pltpu.make_async_copy(source.at[rows, :], target.at[rows, :], sent.at[which, tile])
        for which, (source, target) in enumerate(pairs)
    ]


def norm_rows(tokens, groups, inverse, slope, filtered, query, grad, gain, normed, grad_query):
    def finish(first, group):
        rows = pl.ds(first, ROWS16)
        part = load_dense(filtered, group, first, tokens)
        gated = tile_of(query, first, group) * part
        gains = gain[:, lanes_of(group)]
        scale = inverse[rows, :]
        normed[rows, lanes_of(group)] = (gated * gains * scale).astype(bf16)
        grad_gated = gains * tile_of(grad, first, group) * scale - gated * slope[rows, :]
        grad_query[rows, lanes_of(group)] = (grad_gated * part).astype(bf16)

    each_tile(0, tokens // ROWS16, groups, finish)


def chip_total_and_sum(half, chips, whole, keep, recv, total):
    core = lax.axis_index("core")
    mine, other = keep[0], recv[0]
    farther = jnp.where(core == 1, mine, other)
    nearer = jnp.where(core == 1, other, mine)
    cut = half // chips
    total[:, 0] = (whole[...] * farther + nearer).reshape(chips, cut, LANES)
    total[:, 1] = (keep[1] + recv[1]).reshape(chips, cut, LANES)


def chip_scan_and_sum(chips, whole_cut, totals, before):
    ratio = whole_cut[lax.axis_index(CHIP_AXES)]
    ratio = ratio * ratio

    def step(turn, carried):
        state, total = carried
        at = chips - 1 - turn
        before[at, 0] = state
        return ratio * state + totals[at, 0], total + totals[at, 1]

    zero = jnp.zeros_like(ratio)
    _, total = lax.fori_loop(0, chips, step, (zero, zero), unroll=8)
    before[:, 1] = jnp.broadcast_to(total[None], before[:, 1].shape)


def core_states_and_sum(half, whole, chip_state, keep, recv, mine, other):
    core = lax.axis_index("core")
    farther = jnp.where(core == 1, keep[0], recv[0])
    first = chip_state[:, 0].reshape(half, LANES)
    second = whole[...] * first + farther
    mine[0] = jnp.where(core == 1, first, second)
    other[0] = jnp.where(core == 1, second, first)
    summed = chip_state[:, 1].reshape(half, LANES)
    mine[1] = summed
    other[1] = summed


def grad_mine(tokens, groups, grad_filtered, local_adjoints, shrink, weight, after, partial):
    steps = tokens // STEP
    for block in range(groups // SUB):
        rising, passed = powers(core_half(shrink, block, groups, True), core_half(weight, block, groups, True))
        tap = taps(shrink, weight, block, groups)

        def advance(step, entering):
            states = [s + e for s, e in zip(boundary(local_adjoints, block, step, steps, True), entering)]
            rows = [grad_filtered[token_row(block, step * STEP + inner, tokens), :] for inner in range(STEP)]
            for inner in range(STEP):
                own = [tap[on - inner] * rows[on] for on in range(inner, STEP)]
                partial[token_row(block, step * STEP + inner, tokens), :] = tree_sum(
                    [w * s for w, s in zip(rising[STEP - 1 - inner], states)] + own
                )
            return [p * e for p, e in zip(passed, entering)]

        over_steps(0, steps, 4, advance, half_of(after.at[0], block, groups), backward=True)


def grad_rows(tokens, groups, local_adjoints, shrink, weight, after_mine, after_other, partial, key, value, normed, grad_query,
              grad_key, grad_value, grad_residue, normed_out, grad_query_out,
              total, dense, factors, key_out, value_out, residue_out, sent, whole_sent):
    half = HALF_MODES * groups
    core = lax.axis_index("core")
    total[my_rows(half), :] = after_mine[1]
    total[pl.ds(pl.multiple_of((1 - core) * half, half), half), :] = after_other[1]
    for group in range(groups):
        residue_out[:, lanes_of(group)] = total[pl.ds(group, MODES, stride=groups), :]
    whole_copies = [
        pltpu.make_async_copy(source, target, whole_sent.at[which])
        for which, (source, target) in enumerate(
            ((normed, normed_out), (grad_query, grad_query_out), (residue_out, grad_residue))
        )
    ]
    for copy in whole_copies:
        copy.start()
    blocks = groups // SUB
    tiles = tokens // ROWS16

    pairs = ((key_out, grad_key), (value_out, grad_value))

    for block in range(blocks):
        rising, passed = powers(core_half(shrink, block, groups, False), core_half(weight, block, groups, False))
        for power, values in enumerate(rising + [passed]):
            for mode in range(HALF_MODES):
                factors[block, power, mode] = values[mode]

    def chunk(turn, states):
        tile = tiles - 1 - turn
        first = pl.multiple_of(tile * ROWS16, ROWS16)
        rows = pl.ds(first, ROWS16)
        states = [list(part) for part in states]
        for block in range(blocks):
            *rising, passed = [[factors[block, power, mode] for mode in range(HALF_MODES)] for power in range(STEP + 1)]
            for step in range(ROWS16 // STEP - 1, -1, -1):
                local = boundary(local_adjoints, block, tile * (ROWS16 // STEP) + step, tokens // STEP, False)
                behind = [s + e for s, e in zip(local, states[block])]
                for inner in range(STEP):
                    token = step * STEP + inner
                    part = tree_sum([w * s for w, s in zip(rising[STEP - 1 - inner], behind)])
                    part = part + partial[token_row(block, first + token, tokens), :]
                    dense[block, token * SUB : (token + 1) * SUB, :] = part
                states[block] = [p * e for p, e in zip(passed, states[block])]
            for group in range(block * SUB, (block + 1) * SUB):
                part = dense[block, pl.ds(group % SUB, ROWS16, stride=SUB), :]
                key_out[rows, lanes_of(group)] = (part * tile_of(value, first, group)).astype(bf16)
                value_out[rows, lanes_of(group)] = (part * tile_of(key, first, group)).astype(bf16)
        for copy in tile_copies(tile, sent, *pairs):
            copy.start()
        return states

    lax.fori_loop(0, tiles, chunk, [half_of(after_other.at[0], block, groups) for block in range(blocks)])
    for tile in range(tiles):
        for copy in tile_copies(tile, sent, *pairs):
            copy.wait()
    for copy in whole_copies:
        copy.wait()


def swap(value, axis):
    return lax.ppermute(value, axis, [(0, 1), (1, 0)])


def on_device(query_rows, key_rows, value_rows, decay_rate, residue, norm_gain, grad_out):
    tokens, channels = query_rows.shape
    groups = channels // LANES
    half = HALF_MODES * groups
    chips = lax.axis_size(CHIP_AXES)
    cut = half // chips
    natural = shaped(tokens, channels, dtype=bf16)
    rates = shaped(MODES, channels)
    dense = shaped(tokens * groups + SUB, LANES)
    modal = shaped(2 * half + groups, LANES)
    halved = shaped(half, LANES)
    boundaries = shaped(tokens // STEP * 2 * half, LANES)
    two_halves = shaped(2, half, LANES)
    square = shaped(tokens, LANES)
    modal_scratch = pltpu.VMEM((2 * half + groups, LANES), f32)
    natural_scratch = pltpu.VMEM((tokens, channels), bf16)
    token_scratch = pltpu.VMEM((tokens * SUB + SUB, LANES), f32)
    bind = functools.partial

    inputs = (key_rows, value_rows, decay_rate, residue, norm_gain[None, :])
    product, local_states, keep, send, shrink, whole, key_near, value_near, rate_near, residue_near, gain = call(
        bind(local_ends, tokens, groups),
        (dense, boundaries, halved, halved, modal, halved, natural, natural, rates, rates, shaped(1, channels)),
        *[pltpu.with_memory_space_constraint(array, pltpu.HBM) for array in inputs],
        in_specs=[in_hbm] * len(inputs),
        scratch=[modal_scratch, pltpu.SemaphoreType.DMA((2 * len(CHUNKS) + 3,))],
    )
    whole_cut = whole.reshape(chips, cut, LANES)
    recv = swap(send, "core")
    asked, squared, weight, scale_dense = call(
        bind(prepare, tokens, groups), (dense, dense, modal, modal), query_rows, grad_out, gain, rate_near, residue_near
    )
    recv, asked = lax.optimization_barrier((recv, asked))
    total = call(chip_total, halved, whole, keep, recv)
    totals = lax.all_to_all(total.reshape(chips, cut, LANES), CHIP_AXES, 0, 0)
    before = call(bind(chip_scan, chips), shaped(chips, cut, LANES), whole_cut, totals)
    chip_state = lax.all_to_all(before, CHIP_AXES, 0, 0).reshape(half, LANES)
    entry_mine, entry_send = call(core_states, (halved, halved), whole, chip_state, keep, recv)
    entry_other = swap(entry_send, "core")

    partial = call(bind(filter_mine, tokens, groups), dense, product, local_states, shrink, weight, entry_mine)
    filtered, curved, sums = call(
        bind(filter_other, tokens, groups),
        (dense, dense, shaped(2, tokens)),
        local_states, shrink, weight, entry_other, partial, asked, squared,
        scratch=[token_scratch, token_scratch],
    )
    other_sums = swap(sums, "tp")
    product, sums = lax.optimization_barrier((product, sums))
    product_sums = call(bind(step_sums, tokens, groups), boundaries, product, shrink)

    inverse, slope, grad_filtered, local_adjoints, keep, send = call(
        bind(local_adjoint, tokens, groups),
        (square, square, dense, boundaries, two_halves, two_halves),
        sums, other_sums, asked, curved, product, product_sums, shrink, scale_dense, entry_mine, entry_other,
    )
    recv = swap(send, "core")
    normed_near, grad_query_near = call(
        bind(norm_rows, tokens, groups), (natural, natural), inverse, slope, filtered, query_rows, grad_out, gain
    )
    recv, normed_near, grad_query_near = lax.optimization_barrier((recv, normed_near, grad_query_near))
    total = call(bind(chip_total_and_sum, half, chips), shaped(chips, 2, cut, LANES), whole, keep, recv)
    totals = lax.all_to_all(total, CHIP_AXES, 0, 0)
    before = call(bind(chip_scan_and_sum, chips), shaped(chips, 2, cut, LANES), whole_cut, totals)
    chip_state = lax.all_to_all(before, CHIP_AXES, 0, 0)
    after_mine, after_send = call(
        bind(core_states_and_sum, half), (two_halves, two_halves), whole, chip_state, keep, recv
    )
    after_other = swap(after_send, "core")

    partial = call(bind(grad_mine, tokens, groups), dense, grad_filtered, local_adjoints, shrink, weight, after_mine)
    grad_key, grad_value, grad_residue, normed_out, grad_query = call(
        bind(grad_rows, tokens, groups),
        (natural, natural, rates, natural, natural),
        local_adjoints, shrink, weight, after_mine, after_other, partial, key_near, value_near, normed_near, grad_query_near,
        out_specs=(in_hbm,) * 5,
        scratch=[
            modal_scratch, pltpu.VMEM((groups // SUB, ROWS16 * SUB + SUB, LANES), f32),
            pltpu.VMEM((groups // SUB, STEP + 1, HALF_MODES, SUB, LANES), f32), natural_scratch, natural_scratch,
            pltpu.VMEM((MODES, channels), f32), pltpu.SemaphoreType.DMA((2, tokens // ROWS16)), pltpu.SemaphoreType.DMA((3,)),
        ],
    )
    return (normed_out, grad_query, grad_key, grad_value, grad_residue)


def solution(mesh):
    devices = mesh.devices
    cut_mesh = Mesh(devices.reshape(CTX_SIZES + (devices.shape[1],)), CTX_AXES + ("tp",))
    token_split = P(CTX_AXES, "tp")
    return jax.shard_map(
        on_device,
        mesh=cut_mesh,
        in_specs=(token_split, token_split, token_split, P(None, "tp"), P(None, "tp"), P("tp"), token_split),
        out_specs=(token_split, token_split, token_split, token_split, P(None, "tp")),
        check_vma=False,
    )
```

```python
import functools

import jax
import jax.numpy as jnp
from jax import lax
from jax.experimental import pallas as pl
from jax.experimental.pallas import tpu as pltpu
from jax.sharding import Mesh, PartitionSpec as P

D = 8192
MODES = 8
HALF_MODES = MODES // 2
norm_eps = 1e-05

LANES = 128
SUB = 8
ROWS16 = 16
STEP = 4
CHUNKS = ((0, 2), (2, 8))

CHIP_AXES = ("x", "yl", "z")
CTX_AXES = CHIP_AXES + ("core",)
CTX_SIZES = (4, 2, 8, 2)

f32 = jnp.float32
bf16 = jnp.bfloat16

in_vmem = pl.BlockSpec(memory_space=pltpu.VMEM)
in_hbm = pl.BlockSpec(memory_space=pltpu.HBM)


def call(body, out_shape, *args, scratch=(), in_specs=None, out_specs=None):
    return pl.pallas_call(
        body,
        out_shape=out_shape,
        in_specs=in_specs or [in_vmem] * len(args),
        out_specs=out_specs or jax.tree.map(lambda _: in_vmem, out_shape),
        scratch_shapes=list(scratch),
        compiler_params=pltpu.CompilerParams(vmem_limit_bytes=20 * 1024 * 1024),
    )(*args)


def shaped(*extent, dtype=f32):
    return jax.ShapeDtypeStruct(extent, dtype)


def dense_rows(group, first, tokens):
    return pl.ds(((group // SUB) * tokens + first) * SUB + group % SUB, SUB, stride=SUB)


def each_tile(first_tile, tiles, groups, body):
    def rows(tile, nothing):
        first = pl.multiple_of(tile * ROWS16, ROWS16)
        for group in range(groups):
            body(first, group)
        return nothing

    lax.fori_loop(first_tile, first_tile + tiles, rows, 0)


def load_dense(ref, group, first, tokens):
    return jnp.concatenate(
        [ref[dense_rows(group, first + shift, tokens), :] for shift in (0, SUB)], axis=0
    )


def store_dense(ref, group, first, tokens, value):
    for shift in (0, SUB):
        ref[dense_rows(group, first + shift, tokens), :] = value[shift : shift + SUB]


def lanes_of(group):
    return pl.ds(group * LANES, LANES)


def tile_of(ref, first, group):
    return ref[pl.ds(first, ROWS16), lanes_of(group)].astype(f32)


def half_rows(block, mode, groups):
    return pl.ds(mode * groups + block * SUB, SUB)


def half_of(ref, block, groups):
    return [ref[half_rows(block, mode, groups), :] for mode in range(HALF_MODES)]


def core_half(ref, block, groups, mine):
    core = lax.axis_index("core")
    first = (core if mine else 1 - core) * (HALF_MODES * groups)
    return [
        ref[pl.ds(pl.multiple_of(first + mode * groups + block * SUB, SUB), SUB), :]
        for mode in range(HALF_MODES)
    ]


def both_halves(ref, block, groups):
    return core_half(ref, block, groups, True) + core_half(ref, block, groups, False)


def my_rows(half):
    return pl.ds(pl.multiple_of(lax.axis_index("core") * half, half), half)


def tree_sum(terms):
    while len(terms) > 1:
        pairs = [a + b for a, b in zip(terms[::2], terms[1::2])]
        terms = pairs + terms[len(pairs) * 2 :]
    return terms[0]


def over_steps(first, count, together, body, carried, backward=False):
    def several(turn, carried):
        for inner in range(together):
            at = turn * together + inner
            carried = body(first + (count - 1 - at if backward else at), carried)
        return carried

    return lax.fori_loop(0, count // together, several, carried)


def step_rows(block, step, mode, steps):
    return pl.ds(pl.multiple_of(((block * steps + step) * MODES + mode) * SUB, SUB), SUB)


def boundary(ref, block, step, steps, mine):
    modes = range(HALF_MODES) if mine else range(HALF_MODES, MODES)
    return [ref[step_rows(block, step, mode, steps), :] for mode in modes]


def put_boundary(ref, block, step, steps, states):
    for mode in range(MODES):
        ref[step_rows(block, step, mode, steps), :] = states[mode]


def powers(ratio, factor):
    rising, passed = [factor], ratio
    for turn in range(STEP):
        rising.append([f * r for f, r in zip(rising[-1], ratio)])
        if turn:
            passed = [p * r for p, r in zip(passed, ratio)]
    return rising[1:], passed


def taps(shrink, weight, block, groups):
    ratio, now = both_halves(shrink, block, groups), both_halves(weight, block, groups)
    result = []
    for _ in range(STEP):
        result.append(tree_sum(now))
        now = [n * r for n, r in zip(now, ratio)]
    return result


def token_row(block, token, tokens):
    return pl.ds(pl.multiple_of((block * tokens + token) * SUB, SUB), SUB)


def zero_states(count):
    return [jnp.zeros((SUB, LANES), f32)] * count


def local_ends(tokens, groups, key, value, decay, residue, gain,
               product, local_states, keep, send, shrink, whole, key_in, value_in, rate_in, residue_in, gain_in, whole_all, arrived):
    rate_copy, *later_copies = [
        pltpu.make_async_copy(source, target, arrived.at[2 * len(CHUNKS) + which])
        for which, (source, target) in enumerate(((decay, rate_in), (residue, residue_in), (gain, gain_in)))
    ]
    rate_copy.start()
    copies = []
    for chunk, (begin, end) in enumerate(CHUNKS):
        rows = pl.ds(begin * tokens // 8, (end - begin) * tokens // 8)
        pair = [
            pltpu.make_async_copy(source.at[rows, :], target.at[rows, :], arrived.at[2 * chunk + which])
            for which, (source, target) in enumerate(((key, key_in), (value, value_in)))
        ]
        for copy in pair:
            copy.start()
        copies.append(pair)
    for copy in later_copies:
        copy.start()
    rate_copy.wait()
    for group in range(groups):
        rows = pl.ds(group, MODES, stride=groups)
        rate = rate_in[:, lanes_of(group)]
        shrink[rows, :] = jnp.exp(-rate)
        whole_all[rows, :] = jnp.exp(-rate * tokens)
    whole[...] = whole_all[my_rows(HALF_MODES * groups), :]

    def multiply(first, group):
        store_dense(product, group, first, tokens, tile_of(key_in, first, group) * tile_of(value_in, first, group))

    for chunk, (begin, end) in enumerate(CHUNKS):
        for copy in copies[chunk]:
            copy.wait()
        first, some = begin * tokens // 8, (end - begin) * tokens // 8
        each_tile(first // ROWS16, some // ROWS16, groups, multiply)
        for block in range(groups // SUB):
            ratio = both_halves(shrink, block, groups)

            def advance(step, states):
                put_boundary(local_states, block, step, tokens // STEP, states)
                for inner in range(STEP):
                    row = product[token_row(block, step * STEP + inner, tokens), :]
                    states = [r * s + row for r, s in zip(ratio, states)]
                return states

            states = half_of(keep, block, groups) + half_of(send, block, groups) if chunk else zero_states(MODES)
            states = over_steps(first // STEP, some // STEP, 4, advance, states)
            for mode in range(HALF_MODES):
                keep[half_rows(block, mode, groups), :] = states[mode]
                send[half_rows(block, mode, groups), :] = states[HALF_MODES + mode]
    for copy in later_copies:
        copy.wait()


def one_minus_exp_of_minus(value):
    series = 1.0 - value / 9.0
    for divisor in range(8, 1, -1):
        series = 1.0 - value / divisor * series
    return jnp.where(value < 0.25, value * series, 1.0 - jnp.exp(-value))


def prepare(tokens, groups, query, grad, gain, decay, residue, asked, squared, weight, scale_dense):
    for group in range(groups):
        rows = pl.ds(group, MODES, stride=groups)
        in_scale = jnp.sqrt(one_minus_exp_of_minus(2.0 * decay[:, lanes_of(group)]))
        scale_dense[rows, :] = in_scale
        weight[rows, :] = in_scale * residue[:, lanes_of(group)]

    def multiply(first, group):
        rows = tile_of(query, first, group)
        store_dense(asked, group, first, tokens, gain[:, lanes_of(group)] * tile_of(grad, first, group) * rows)
        store_dense(squared, group, first, tokens, rows * rows)

    each_tile(0, tokens // ROWS16, groups, multiply)


def chip_total(whole, keep, recv, total):
    mine_is_farther = lax.axis_index("core") == 0
    mine, other = keep[...], recv[...]
    farther = jnp.where(mine_is_farther, mine, other)
    nearer = jnp.where(mine_is_farther, other, mine)
    total[...] = whole[...] * farther + nearer


def chip_scan(chips, whole_cut, totals, before):
    ratio = whole_cut[lax.axis_index(CHIP_AXES)]
    ratio = ratio * ratio

    def step(at, state):
        before[at] = state
        return ratio * state + totals[at]

    lax.fori_loop(0, chips, step, jnp.zeros_like(ratio), unroll=8)


def core_states(whole, chip_state, keep, recv, mine, other):
    mine_is_farther = lax.axis_index("core") == 0
    farther = jnp.where(mine_is_farther, keep[...], recv[...])
    first = chip_state[...]
    second = whole[...] * first + farther
    mine[...] = jnp.where(mine_is_farther, first, second)
    other[...] = jnp.where(mine_is_farther, second, first)


def filter_mine(tokens, groups, product, local_states, shrink, weight, entry, partial):
    steps = tokens // STEP
    for block in range(groups // SUB):
        rising, passed = powers(core_half(shrink, block, groups, True), core_half(weight, block, groups, True))
        tap = taps(shrink, weight, block, groups)

        def advance(step, entering):
            states = [s + e for s, e in zip(boundary(local_states, block, step, steps, True), entering)]
            rows = []
            for inner in range(STEP):
                at = token_row(block, step * STEP + inner, tokens)
                rows.append(product[at, :])
                own = [tap[inner - back] * rows[back] for back in range(inner + 1)]
                partial[at, :] = tree_sum([w * s for w, s in zip(rising[inner], states)] + own)
            return [p * e for p, e in zip(passed, entering)]

        over_steps(0, steps, 4, advance, half_of(entry, block, groups))


def filter_other(tokens, groups, local_states, shrink, weight, entry, partial, asked, squared, filtered, curved, sums, squares, dots):
    steps = tokens // STEP
    for block in range(groups // SUB):
        rising, passed = powers(core_half(shrink, block, groups, False), core_half(weight, block, groups, False))

        def advance(step, entering):
            states = [s + e for s, e in zip(boundary(local_states, block, step, steps, False), entering)]
            for inner in range(STEP):
                token = step * STEP + inner
                at = token_row(block, token, tokens)
                value = tree_sum([w * s for w, s in zip(rising[inner], states)]) + partial[at, :]
                bent = squared[at, :] * value
                filtered[at, :] = value
                curved[at, :] = bent
                rows = token_row(0, token, tokens)
                square_term, dot_term = bent * value, asked[at, :] * value
                squares[rows, :] = square_term + squares[rows, :] if block else square_term
                dots[rows, :] = dot_term + dots[rows, :] if block else dot_term
            return [p * e for p, e in zip(passed, entering)]

        over_steps(0, steps, 4, advance, half_of(entry, block, groups))
    for line, ref in enumerate((squares, dots)):
        per_token = tree_sum([ref[pl.ds(shift, tokens, stride=SUB), :] for shift in range(SUB)])
        sums[line : line + 1, :] = jnp.sum(per_token.T, axis=0, keepdims=True)


def step_sums(tokens, groups, product, shrink, sums):
    steps = tokens // STEP
    for block in range(groups // SUB):
        ratio = both_halves(shrink, block, groups)

        def gather(step, nothing):
            rows = [product[token_row(block, step * STEP + inner, tokens), :] for inner in range(STEP)]
            total = [r * rows[0] for r in ratio]
            for row in rows[1:]:
                total = [r * (row + t) for r, t in zip(ratio, total)]
            put_boundary(sums, block, step, steps, total)
            return nothing

        over_steps(0, steps, 4, gather, 0)


def local_adjoint(tokens, groups, sums, other_sums, asked, curved, product, product_sums, shrink, scale_dense, entry_mine, entry_other,
                  inverse, slope, grad_filtered, local_adjoints, keep, send):
    steps = tokens // STEP
    both = sums[...] + other_sums[...]
    rms = jnp.sqrt(both[0:1] / D + norm_eps)
    inverse[...] = jnp.broadcast_to(1.0 / rms, (LANES, tokens)).T
    slope[...] = jnp.broadcast_to(both[1:2] / (D * rms * rms * rms), (LANES, tokens)).T
    for block in range(groups // SUB):
        ratio = both_halves(shrink, block, groups)

        def advance(step, carried):
            states, terms, shared = carried
            put_boundary(local_adjoints, block, step, steps, states)
            along = boundary(product_sums, block, step, steps, True) + boundary(product_sums, block, step, steps, False)
            terms = [q + a * s for q, a, s in zip(terms, along, states)]
            grads = [None] * STEP
            for inner in range(STEP - 1, -1, -1):
                token = step * STEP + inner
                at = token_row(block, token, tokens)
                now = pl.ds(token, 1)
                grads[inner] = inverse[now, :] * asked[at, :] - slope[now, :] * curved[at, :]
                grad_filtered[at, :] = grads[inner]
                states = [r * s + grads[inner] for r, s in zip(ratio, states)]
                put_in = product[at, :]
                shared = [
                    c + put_in * grads[inner + apart] if inner + apart < STEP else c for apart, c in enumerate(shared)
                ]
            return states, terms, shared

        start = (zero_states(MODES), zero_states(MODES), zero_states(STEP))
        states, terms, shared = over_steps(0, steps, 2, advance, start, backward=True)
        for mode in range(MODES):
            near = shared[STEP - 1]
            for part in shared[STEP - 2 :: -1]:
                near = part + ratio[mode] * near
            terms[mode] = terms[mode] + near
        entry = half_of(entry_mine, block, groups) + half_of(entry_other, block, groups)
        scale = both_halves(scale_dense, block, groups)
        terms = [i * (q + r * s * e) for i, q, r, s, e in zip(scale, terms, ratio, states, entry)]
        for mode in range(HALF_MODES):
            rows = half_rows(block, mode, groups)
            keep[0, rows, :], keep[1, rows, :] = states[mode], terms[mode]
            send[0, rows, :], send[1, rows, :] = states[HALF_MODES + mode], terms[HALF_MODES + mode]


def tile_copies(tile, sent, *pairs):
    rows = pl.ds(pl.multiple_of(tile * ROWS16, ROWS16), ROWS16)
    return [
        pltpu.make_async_copy(source.at[rows, :], target.at[rows, :], sent.at[which, tile])
        for which, (source, target) in enumerate(pairs)
    ]


def norm_rows(tokens, groups, inverse, slope, filtered, query, grad, gain, normed, grad_query):
    def finish(first, group):
        rows = pl.ds(first, ROWS16)
        part = load_dense(filtered, group, first, tokens)
        gated = tile_of(query, first, group) * part
        gains = gain[:, lanes_of(group)]
        scale = inverse[rows, :]
        normed[rows, lanes_of(group)] = (gated * gains * scale).astype(bf16)
        grad_gated = gains * tile_of(grad, first, group) * scale - gated * slope[rows, :]
        grad_query[rows, lanes_of(group)] = (grad_gated * part).astype(bf16)

    each_tile(0, tokens // ROWS16, groups, finish)


def chip_total_and_sum(half, chips, whole, keep, recv, total):
    core = lax.axis_index("core")
    mine, other = keep[0], recv[0]
    farther = jnp.where(core == 1, mine, other)
    nearer = jnp.where(core == 1, other, mine)
    cut = half // chips
    total[:, 0] = (whole[...] * farther + nearer).reshape(chips, cut, LANES)
    total[:, 1] = (keep[1] + recv[1]).reshape(chips, cut, LANES)


def chip_scan_and_sum(chips, whole_cut, totals, before):
    ratio = whole_cut[lax.axis_index(CHIP_AXES)]
    ratio = ratio * ratio

    def step(turn, carried):
        state, total = carried
        at = chips - 1 - turn
        before[at, 0] = state
        return ratio * state + totals[at, 0], total + totals[at, 1]

    zero = jnp.zeros_like(ratio)
    _, total = lax.fori_loop(0, chips, step, (zero, zero), unroll=8)
    before[:, 1] = jnp.broadcast_to(total[None], before[:, 1].shape)


def core_states_and_sum(half, whole, chip_state, keep, recv, mine, other):
    core = lax.axis_index("core")
    farther = jnp.where(core == 1, keep[0], recv[0])
    first = chip_state[:, 0].reshape(half, LANES)
    second = whole[...] * first + farther
    mine[0] = jnp.where(core == 1, first, second)
    other[0] = jnp.where(core == 1, second, first)
    summed = chip_state[:, 1].reshape(half, LANES)
    mine[1] = summed
    other[1] = summed


def grad_mine(tokens, groups, grad_filtered, local_adjoints, shrink, weight, after, normed, partial, normed_out, sent):
    steps = tokens // STEP
    copy = pltpu.make_async_copy(normed, normed_out, sent)
    copy.start()
    for block in range(groups // SUB):
        rising, passed = powers(core_half(shrink, block, groups, True), core_half(weight, block, groups, True))
        tap = taps(shrink, weight, block, groups)

        def advance(step, entering):
            states = [s + e for s, e in zip(boundary(local_adjoints, block, step, steps, True), entering)]
            rows = [grad_filtered[token_row(block, step * STEP + inner, tokens), :] for inner in range(STEP)]
            for inner in range(STEP):
                own = [tap[on - inner] * rows[on] for on in range(inner, STEP)]
                partial[token_row(block, step * STEP + inner, tokens), :] = tree_sum(
                    [w * s for w, s in zip(rising[STEP - 1 - inner], states)] + own
                )
            return [p * e for p, e in zip(passed, entering)]

        over_steps(0, steps, 4, advance, half_of(after.at[0], block, groups), backward=True)
    copy.wait()


def grad_rows(tokens, groups, local_adjoints, shrink, weight, after_mine, after_other, partial, key, value, grad_query,
              grad_key, grad_value, grad_residue, grad_query_out,
              total, dense, factors, key_out, value_out, residue_out, sent, whole_sent):
    half = HALF_MODES * groups
    core = lax.axis_index("core")
    total[my_rows(half), :] = after_mine[1]
    total[pl.ds(pl.multiple_of((1 - core) * half, half), half), :] = after_other[1]
    for group in range(groups):
        residue_out[:, lanes_of(group)] = total[pl.ds(group, MODES, stride=groups), :]
    whole_copies = [
        pltpu.make_async_copy(source, target, whole_sent.at[which])
        for which, (source, target) in enumerate(
            ((grad_query, grad_query_out), (residue_out, grad_residue))
        )
    ]
    for copy in whole_copies:
        copy.start()
    blocks = groups // SUB
    tiles = tokens // ROWS16

    pairs = ((key_out, grad_key), (value_out, grad_value))

    for block in range(blocks):
        rising, passed = powers(core_half(shrink, block, groups, False), core_half(weight, block, groups, False))
        for power, values in enumerate(rising + [passed]):
            for mode in range(HALF_MODES):
                factors[block, power, mode] = values[mode]

    def chunk(turn, states):
        tile = tiles - 1 - turn
        first = pl.multiple_of(tile * ROWS16, ROWS16)
        rows = pl.ds(first, ROWS16)
        states = [list(part) for part in states]
        for block in range(blocks):
            *rising, passed = [[factors[block, power, mode] for mode in range(HALF_MODES)] for power in range(STEP + 1)]
            for step in range(ROWS16 // STEP - 1, -1, -1):
                local = boundary(local_adjoints, block, tile * (ROWS16 // STEP) + step, tokens // STEP, False)
                behind = [s + e for s, e in zip(local, states[block])]
                for inner in range(STEP):
                    token = step * STEP + inner
                    part = tree_sum([w * s for w, s in zip(rising[STEP - 1 - inner], behind)])
                    part = part + partial[token_row(block, first + token, tokens), :]
                    dense[block, token * SUB : (token + 1) * SUB, :] = part
                states[block] = [p * e for p, e in zip(passed, states[block])]
            for group in range(block * SUB, (block + 1) * SUB):
                part = dense[block, pl.ds(group % SUB, ROWS16, stride=SUB), :]
                key_out[rows, lanes_of(group)] = (part * tile_of(value, first, group)).astype(bf16)
                value_out[rows, lanes_of(group)] = (part * tile_of(key, first, group)).astype(bf16)
        for copy in tile_copies(tile, sent, *pairs):
            copy.start()
        return states

    lax.fori_loop(0, tiles, chunk, [half_of(after_other.at[0], block, groups) for block in range(blocks)])
    for tile in range(tiles):
        for copy in tile_copies(tile, sent, *pairs):
            copy.wait()
    for copy in whole_copies:
        copy.wait()


def swap(value, axis):
    return lax.ppermute(value, axis, [(0, 1), (1, 0)])


def on_device(query_rows, key_rows, value_rows, decay_rate, residue, norm_gain, grad_out):
    tokens, channels = query_rows.shape
    groups = channels // LANES
    half = HALF_MODES * groups
    chips = lax.axis_size(CHIP_AXES)
    cut = half // chips
    natural = shaped(tokens, channels, dtype=bf16)
    rates = shaped(MODES, channels)
    dense = shaped(tokens * groups + SUB, LANES)
    modal = shaped(2 * half + groups, LANES)
    halved = shaped(half, LANES)
    boundaries = shaped(tokens // STEP * 2 * half, LANES)
    two_halves = shaped(2, half, LANES)
    square = shaped(tokens, LANES)
    modal_scratch = pltpu.VMEM((2 * half + groups, LANES), f32)
    natural_scratch = pltpu.VMEM((tokens, channels), bf16)
    token_scratch = pltpu.VMEM((tokens * SUB + SUB, LANES), f32)
    bind = functools.partial

    inputs = (key_rows, value_rows, decay_rate, residue, norm_gain[None, :])
    product, local_states, keep, send, shrink, whole, key_near, value_near, rate_near, residue_near, gain = call(
        bind(local_ends, tokens, groups),
        (dense, boundaries, halved, halved, modal, halved, natural, natural, rates, rates, shaped(1, channels)),
        *[pltpu.with_memory_space_constraint(array, pltpu.HBM) for array in inputs],
        in_specs=[in_hbm] * len(inputs),
        scratch=[modal_scratch, pltpu.SemaphoreType.DMA((2 * len(CHUNKS) + 3,))],
    )
    whole_cut = whole.reshape(chips, cut, LANES)
    recv = swap(send, "core")
    asked, squared, weight, scale_dense = call(
        bind(prepare, tokens, groups), (dense, dense, modal, modal), query_rows, grad_out, gain, rate_near, residue_near
    )
    recv, asked = lax.optimization_barrier((recv, asked))
    total = call(chip_total, halved, whole, keep, recv)
    totals = lax.all_to_all(total.reshape(chips, cut, LANES), CHIP_AXES, 0, 0)
    before = call(bind(chip_scan, chips), shaped(chips, cut, LANES), whole_cut, totals)
    chip_state = lax.all_to_all(before, CHIP_AXES, 0, 0).reshape(half, LANES)
    entry_mine, entry_send = call(core_states, (halved, halved), whole, chip_state, keep, recv)
    entry_other = swap(entry_send, "core")

    partial = call(bind(filter_mine, tokens, groups), dense, product, local_states, shrink, weight, entry_mine)
    filtered, curved, sums = call(
        bind(filter_other, tokens, groups),
        (dense, dense, shaped(2, tokens)),
        local_states, shrink, weight, entry_other, partial, asked, squared,
        scratch=[token_scratch, token_scratch],
    )
    other_sums = swap(sums, "tp")
    product, sums = lax.optimization_barrier((product, sums))
    product_sums = call(bind(step_sums, tokens, groups), boundaries, product, shrink)

    inverse, slope, grad_filtered, local_adjoints, keep, send = call(
        bind(local_adjoint, tokens, groups),
        (square, square, dense, boundaries, two_halves, two_halves),
        sums, other_sums, asked, curved, product, product_sums, shrink, scale_dense, entry_mine, entry_other,
    )
    recv = swap(send, "core")
    normed_near, grad_query_near = call(
        bind(norm_rows, tokens, groups), (natural, natural), inverse, slope, filtered, query_rows, grad_out, gain
    )
    recv, normed_near, grad_query_near = lax.optimization_barrier((recv, normed_near, grad_query_near))
    total = call(bind(chip_total_and_sum, half, chips), shaped(chips, 2, cut, LANES), whole, keep, recv)
    totals = lax.all_to_all(total, CHIP_AXES, 0, 0)
    before = call(bind(chip_scan_and_sum, chips), shaped(chips, 2, cut, LANES), whole_cut, totals)
    chip_state = lax.all_to_all(before, CHIP_AXES, 0, 0)
    after_mine, after_send = call(
        bind(core_states_and_sum, half), (two_halves, two_halves), whole, chip_state, keep, recv
    )
    after_other = swap(after_send, "core")

    partial, normed_out = call(
        bind(grad_mine, tokens, groups),
        (dense, natural),
        grad_filtered, local_adjoints, shrink, weight, after_mine, normed_near,
        out_specs=(in_vmem, in_hbm),
        scratch=[pltpu.SemaphoreType.DMA],
    )
    grad_key, grad_value, grad_residue, grad_query = call(
        bind(grad_rows, tokens, groups),
        (natural, natural, rates, natural),
        local_adjoints, shrink, weight, after_mine, after_other, partial, key_near, value_near, grad_query_near,
        out_specs=(in_hbm,) * 4,
        scratch=[
            modal_scratch, pltpu.VMEM((groups // SUB, ROWS16 * SUB + SUB, LANES), f32),
            pltpu.VMEM((groups // SUB, STEP + 1, HALF_MODES, SUB, LANES), f32), natural_scratch, natural_scratch,
            pltpu.VMEM((MODES, channels), f32), pltpu.SemaphoreType.DMA((2, tokens // ROWS16)), pltpu.SemaphoreType.DMA((2,)),
        ],
    )
    return (normed_out, grad_query, grad_key, grad_value, grad_residue)


def solution(mesh):
    devices = mesh.devices
    cut_mesh = Mesh(devices.reshape(CTX_SIZES + (devices.shape[1],)), CTX_AXES + ("tp",))
    token_split = P(CTX_AXES, "tp")
    return jax.shard_map(
        on_device,
        mesh=cut_mesh,
        in_specs=(token_split, token_split, token_split, P(None, "tp"), P(None, "tp"), P("tp"), token_split),
        out_specs=(token_split, token_split, token_split, token_split, P(None, "tp")),
        check_vma=False,
    )
```

```python
import functools

import jax
import jax.numpy as jnp
from jax import lax
from jax.experimental import pallas as pl
from jax.experimental.pallas import tpu as pltpu
from jax.sharding import Mesh, PartitionSpec as P

D = 8192
MODES = 8
HALF_MODES = MODES // 2
norm_eps = 1e-05

LANES = 128
SUB = 8
ROWS16 = 16
STEP = 4
CHUNKS = ((0, 2), (2, 8))

CHIP_AXES = ("x", "yl", "z")
CTX_AXES = CHIP_AXES + ("core",)
CTX_SIZES = (4, 2, 8, 2)

f32 = jnp.float32
bf16 = jnp.bfloat16

in_vmem = pl.BlockSpec(memory_space=pltpu.VMEM)
in_hbm = pl.BlockSpec(memory_space=pltpu.HBM)


def call(body, out_shape, *args, scratch=(), in_specs=None, out_specs=None):
    return pl.pallas_call(
        body,
        out_shape=out_shape,
        in_specs=in_specs or [in_vmem] * len(args),
        out_specs=out_specs or jax.tree.map(lambda _: in_vmem, out_shape),
        scratch_shapes=list(scratch),
        compiler_params=pltpu.CompilerParams(vmem_limit_bytes=20 * 1024 * 1024),
    )(*args)


def shaped(*extent, dtype=f32):
    return jax.ShapeDtypeStruct(extent, dtype)


def dense_rows(group, first, tokens):
    return pl.ds(((group // SUB) * tokens + first) * SUB + group % SUB, SUB, stride=SUB)


def each_tile(first_tile, tiles, groups, body):
    def rows(tile, nothing):
        first = pl.multiple_of(tile * ROWS16, ROWS16)
        for group in range(groups):
            body(first, group)
        return nothing

    lax.fori_loop(first_tile, first_tile + tiles, rows, 0)


def load_dense(ref, group, first, tokens):
    return jnp.concatenate(
        [ref[dense_rows(group, first + shift, tokens), :] for shift in (0, SUB)], axis=0
    )


def store_dense(ref, group, first, tokens, value):
    for shift in (0, SUB):
        ref[dense_rows(group, first + shift, tokens), :] = value[shift : shift + SUB]


def lanes_of(group):
    return pl.ds(group * LANES, LANES)


def tile_of(ref, first, group):
    return ref[pl.ds(first, ROWS16), lanes_of(group)].astype(f32)


def half_rows(block, mode, groups):
    return pl.ds(mode * groups + block * SUB, SUB)


def half_of(ref, block, groups):
    return [ref[half_rows(block, mode, groups), :] for mode in range(HALF_MODES)]


def core_half(ref, block, groups, mine):
    core = lax.axis_index("core")
    first = (core if mine else 1 - core) * (HALF_MODES * groups)
    return [
        ref[pl.ds(pl.multiple_of(first + mode * groups + block * SUB, SUB), SUB), :]
        for mode in range(HALF_MODES)
    ]


def both_halves(ref, block, groups):
    return core_half(ref, block, groups, True) + core_half(ref, block, groups, False)


def my_rows(half):
    return pl.ds(pl.multiple_of(lax.axis_index("core") * half, half), half)


def tree_sum(terms):
    while len(terms) > 1:
        pairs = [a + b for a, b in zip(terms[::2], terms[1::2])]
        terms = pairs + terms[len(pairs) * 2 :]
    return terms[0]


def over_steps(first, count, together, body, carried, backward=False):
    def several(turn, carried):
        for inner in range(together):
            at = turn * together + inner
            carried = body(first + (count - 1 - at if backward else at), carried)
        return carried

    return lax.fori_loop(0, count // together, several, carried)


def step_rows(block, step, mode, steps):
    return pl.ds(pl.multiple_of(((block * steps + step) * MODES + mode) * SUB, SUB), SUB)


def boundary(ref, block, step, steps, mine):
    modes = range(HALF_MODES) if mine else range(HALF_MODES, MODES)
    return [ref[step_rows(block, step, mode, steps), :] for mode in modes]


def put_boundary(ref, block, step, steps, states):
    for mode in range(MODES):
        ref[step_rows(block, step, mode, steps), :] = states[mode]


def powers(ratio, factor):
    rising, passed = [factor], ratio
    for turn in range(STEP):
        rising.append([f * r for f, r in zip(rising[-1], ratio)])
        if turn:
            passed = [p * r for p, r in zip(passed, ratio)]
    return rising[1:], passed


def taps(shrink, weight, block, groups):
    ratio, now = both_halves(shrink, block, groups), both_halves(weight, block, groups)
    result = []
    for _ in range(STEP):
        result.append(tree_sum(now))
        now = [n * r for n, r in zip(now, ratio)]
    return result


def token_row(block, token, tokens):
    return pl.ds(pl.multiple_of((block * tokens + token) * SUB, SUB), SUB)


def zero_states(count):
    return [jnp.zeros((SUB, LANES), f32)] * count


def local_ends(tokens, groups, key, value, decay, residue, gain,
               product, local_states, keep, send, shrink, whole, key_in, value_in, rate_in, residue_in, gain_in, whole_all, arrived):
    rate_copy, *later_copies = [
        pltpu.make_async_copy(source, target, arrived.at[2 * len(CHUNKS) + which])
        for which, (source, target) in enumerate(((decay, rate_in), (residue, residue_in), (gain, gain_in)))
    ]
    rate_copy.start()
    copies = []
    for chunk, (begin, end) in enumerate(CHUNKS):
        rows = pl.ds(begin * tokens // 8, (end - begin) * tokens // 8)
        pair = [
            pltpu.make_async_copy(source.at[rows, :], target.at[rows, :], arrived.at[2 * chunk + which])
            for which, (source, target) in enumerate(((key, key_in), (value, value_in)))
        ]
        for copy in pair:
            copy.start()
        copies.append(pair)
    for copy in later_copies:
        copy.start()
    rate_copy.wait()
    for group in range(groups):
        rows = pl.ds(group, MODES, stride=groups)
        rate = rate_in[:, lanes_of(group)]
        shrink[rows, :] = jnp.exp(-rate)
        whole_all[rows, :] = jnp.exp(-rate * tokens)
    whole[...] = whole_all[my_rows(HALF_MODES * groups), :]

    def multiply(first, group):
        store_dense(product, group, first, tokens, tile_of(key_in, first, group) * tile_of(value_in, first, group))

    for chunk, (begin, end) in enumerate(CHUNKS):
        for copy in copies[chunk]:
            copy.wait()
        first, some = begin * tokens // 8, (end - begin) * tokens // 8
        each_tile(first // ROWS16, some // ROWS16, groups, multiply)
        for block in range(groups // SUB):
            ratio = both_halves(shrink, block, groups)

            def advance(step, states):
                put_boundary(local_states, block, step, tokens // STEP, states)
                for inner in range(STEP):
                    row = product[token_row(block, step * STEP + inner, tokens), :]
                    states = [r * s + row for r, s in zip(ratio, states)]
                return states

            states = half_of(keep, block, groups) + half_of(send, block, groups) if chunk else zero_states(MODES)
            states = over_steps(first // STEP, some // STEP, 4, advance, states)
            for mode in range(HALF_MODES):
                keep[half_rows(block, mode, groups), :] = states[mode]
                send[half_rows(block, mode, groups), :] = states[HALF_MODES + mode]
    for copy in later_copies:
        copy.wait()


def one_minus_exp_of_minus(value):
    series = 1.0 - value / 9.0
    for divisor in range(8, 1, -1):
        series = 1.0 - value / divisor * series
    return jnp.where(value < 0.25, value * series, 1.0 - jnp.exp(-value))


def prepare(tokens, groups, query, grad, gain, decay, residue, asked, squared, weight, scale_dense):
    for group in range(groups):
        rows = pl.ds(group, MODES, stride=groups)
        in_scale = jnp.sqrt(one_minus_exp_of_minus(2.0 * decay[:, lanes_of(group)]))
        scale_dense[rows, :] = in_scale
        weight[rows, :] = in_scale * residue[:, lanes_of(group)]

    def multiply(first, group):
        rows = tile_of(query, first, group)
        store_dense(asked, group, first, tokens, gain[:, lanes_of(group)] * tile_of(grad, first, group) * rows)
        store_dense(squared, group, first, tokens, rows * rows)

    each_tile(0, tokens // ROWS16, groups, multiply)


def chip_total(whole, keep, recv, total):
    mine_is_farther = lax.axis_index("core") == 0
    mine, other = keep[...], recv[...]
    farther = jnp.where(mine_is_farther, mine, other)
    nearer = jnp.where(mine_is_farther, other, mine)
    total[...] = whole[...] * farther + nearer


def chip_scan(chips, whole_cut, totals, before):
    ratio = whole_cut[lax.axis_index(CHIP_AXES)]
    ratio = ratio * ratio

    def step(at, state):
        before[at] = state
        return ratio * state + totals[at]

    lax.fori_loop(0, chips, step, jnp.zeros_like(ratio), unroll=8)


def core_states(whole, chip_state, keep, recv, mine, other):
    mine_is_farther = lax.axis_index("core") == 0
    farther = jnp.where(mine_is_farther, keep[...], recv[...])
    first = chip_state[...]
    second = whole[...] * first + farther
    mine[...] = jnp.where(mine_is_farther, first, second)
    other[...] = jnp.where(mine_is_farther, second, first)


def filter_mine(tokens, groups, product, local_states, shrink, weight, entry, partial):
    steps = tokens // STEP
    for block in range(groups // SUB):
        rising, passed = powers(core_half(shrink, block, groups, True), core_half(weight, block, groups, True))
        tap = taps(shrink, weight, block, groups)

        def advance(step, entering):
            states = [s + e for s, e in zip(boundary(local_states, block, step, steps, True), entering)]
            rows = []
            for inner in range(STEP):
                at = token_row(block, step * STEP + inner, tokens)
                rows.append(product[at, :])
                own = [tap[inner - back] * rows[back] for back in range(inner + 1)]
                partial[at, :] = tree_sum([w * s for w, s in zip(rising[inner], states)] + own)
            return [p * e for p, e in zip(passed, entering)]

        over_steps(0, steps, 4, advance, half_of(entry, block, groups))


def filter_other(tokens, groups, local_states, shrink, weight, entry, partial, asked, squared, filtered, curved, sums, squares, dots):
    steps = tokens // STEP
    for block in range(groups // SUB):
        rising, passed = powers(core_half(shrink, block, groups, False), core_half(weight, block, groups, False))

        def advance(step, entering):
            states = [s + e for s, e in zip(boundary(local_states, block, step, steps, False), entering)]
            for inner in range(STEP):
                token = step * STEP + inner
                at = token_row(block, token, tokens)
                value = tree_sum([w * s for w, s in zip(rising[inner], states)]) + partial[at, :]
                bent = squared[at, :] * value
                filtered[at, :] = value
                curved[at, :] = bent
                rows = token_row(0, token, tokens)
                square_term, dot_term = bent * value, asked[at, :] * value
                squares[rows, :] = square_term + squares[rows, :] if block else square_term
                dots[rows, :] = dot_term + dots[rows, :] if block else dot_term
            return [p * e for p, e in zip(passed, entering)]

        over_steps(0, steps, 4, advance, half_of(entry, block, groups))
    for line, ref in enumerate((squares, dots)):
        per_token = tree_sum([ref[pl.ds(shift, tokens, stride=SUB), :] for shift in range(SUB)])
        sums[line : line + 1, :] = jnp.sum(per_token.T, axis=0, keepdims=True)


def step_sums(tokens, groups, product, shrink, sums):
    steps = tokens // STEP
    for block in range(groups // SUB):
        ratio = both_halves(shrink, block, groups)

        def gather(step, nothing):
            rows = [product[token_row(block, step * STEP + inner, tokens), :] for inner in range(STEP)]
            total = [r * rows[0] for r in ratio]
            for row in rows[1:]:
                total = [r * (row + t) for r, t in zip(ratio, total)]
            put_boundary(sums, block, step, steps, total)
            return nothing

        over_steps(0, steps, 4, gather, 0)


def local_adjoint(tokens, groups, sums, other_sums, asked, curved, product, product_sums, shrink, scale_dense, entry_mine, entry_other,
                  inverse, slope, grad_filtered, local_adjoints, keep, send):
    steps = tokens // STEP
    both = sums[...] + other_sums[...]
    rms = jnp.sqrt(both[0:1] / D + norm_eps)
    inverse[...] = jnp.broadcast_to(1.0 / rms, (LANES, tokens)).T
    slope[...] = jnp.broadcast_to(both[1:2] / (D * rms * rms * rms), (LANES, tokens)).T
    for block in range(groups // SUB):
        ratio = both_halves(shrink, block, groups)

        def advance(step, carried):
            states, terms, shared = carried
            put_boundary(local_adjoints, block, step, steps, states)
            along = boundary(product_sums, block, step, steps, True) + boundary(product_sums, block, step, steps, False)
            terms = [q + a * s for q, a, s in zip(terms, along, states)]
            grads = [None] * STEP
            for inner in range(STEP - 1, -1, -1):
                token = step * STEP + inner
                at = token_row(block, token, tokens)
                now = pl.ds(token, 1)
                grads[inner] = inverse[now, :] * asked[at, :] - slope[now, :] * curved[at, :]
                grad_filtered[at, :] = grads[inner]
                states = [r * s + grads[inner] for r, s in zip(ratio, states)]
                put_in = product[at, :]
                shared = [
                    c + put_in * grads[inner + apart] if inner + apart < STEP else c for apart, c in enumerate(shared)
                ]
            return states, terms, shared

        start = (zero_states(MODES), zero_states(MODES), zero_states(STEP))
        states, terms, shared = over_steps(0, steps, 2, advance, start, backward=True)
        for mode in range(MODES):
            near = shared[STEP - 1]
            for part in shared[STEP - 2 :: -1]:
                near = part + ratio[mode] * near
            terms[mode] = terms[mode] + near
        entry = half_of(entry_mine, block, groups) + half_of(entry_other, block, groups)
        scale = both_halves(scale_dense, block, groups)
        terms = [i * (q + r * s * e) for i, q, r, s, e in zip(scale, terms, ratio, states, entry)]
        for mode in range(HALF_MODES):
            rows = half_rows(block, mode, groups)
            keep[0, rows, :], keep[1, rows, :] = states[mode], terms[mode]
            send[0, rows, :], send[1, rows, :] = states[HALF_MODES + mode], terms[HALF_MODES + mode]


def tile_copies(tile, sent, *pairs):
    rows = pl.ds(pl.multiple_of(tile * ROWS16, ROWS16), ROWS16)
    return [
        pltpu.make_async_copy(source.at[rows, :], target.at[rows, :], sent.at[which, tile])
        for which, (source, target) in enumerate(pairs)
    ]


def norm_rows(tokens, groups, inverse, slope, filtered, query, grad, gain, normed, grad_query):
    def finish(first, group):
        rows = pl.ds(first, ROWS16)
        part = load_dense(filtered, group, first, tokens)
        gated = tile_of(query, first, group) * part
        gains = gain[:, lanes_of(group)]
        scale = inverse[rows, :]
        normed[rows, lanes_of(group)] = (gated * gains * scale).astype(bf16)
        grad_gated = gains * tile_of(grad, first, group) * scale - gated * slope[rows, :]
        grad_query[rows, lanes_of(group)] = (grad_gated * part).astype(bf16)

    each_tile(0, tokens // ROWS16, groups, finish)


def chip_total_and_sum(half, chips, whole, keep, recv, total):
    core = lax.axis_index("core")
    mine, other = keep[0], recv[0]
    farther = jnp.where(core == 1, mine, other)
    nearer = jnp.where(core == 1, other, mine)
    cut = half // chips
    total[:, 0] = (whole[...] * farther + nearer).reshape(chips, cut, LANES)
    total[:, 1] = (keep[1] + recv[1]).reshape(chips, cut, LANES)


def chip_scan_and_sum(chips, whole_cut, totals, before):
    ratio = whole_cut[lax.axis_index(CHIP_AXES)]
    ratio = ratio * ratio

    def step(turn, carried):
        state, total = carried
        at = chips - 1 - turn
        before[at, 0] = state
        return ratio * state + totals[at, 0], total + totals[at, 1]

    zero = jnp.zeros_like(ratio)
    _, total = lax.fori_loop(0, chips, step, (zero, zero), unroll=8)
    before[:, 1] = jnp.broadcast_to(total[None], before[:, 1].shape)


def core_states_and_sum(half, whole, chip_state, keep, recv, mine, other):
    core = lax.axis_index("core")
    farther = jnp.where(core == 1, keep[0], recv[0])
    first = chip_state[:, 0].reshape(half, LANES)
    second = whole[...] * first + farther
    mine[0] = jnp.where(core == 1, first, second)
    other[0] = jnp.where(core == 1, second, first)
    summed = chip_state[:, 1].reshape(half, LANES)
    mine[1] = summed
    other[1] = summed


def grad_mine(tokens, groups, grad_filtered, local_adjoints, shrink, weight, after, normed, partial, normed_out, sent):
    steps = tokens // STEP
    copy = pltpu.make_async_copy(normed, normed_out, sent)
    copy.start()
    for block in range(groups // SUB):
        rising, passed = powers(core_half(shrink, block, groups, True), core_half(weight, block, groups, True))
        tap = taps(shrink, weight, block, groups)

        def advance(step, entering):
            states = [s + e for s, e in zip(boundary(local_adjoints, block, step, steps, True), entering)]
            rows = [grad_filtered[token_row(block, step * STEP + inner, tokens), :] for inner in range(STEP)]
            for inner in range(STEP):
                own = [tap[on - inner] * rows[on] for on in range(inner, STEP)]
                partial[token_row(block, step * STEP + inner, tokens), :] = tree_sum(
                    [w * s for w, s in zip(rising[STEP - 1 - inner], states)] + own
                )
            return [p * e for p, e in zip(passed, entering)]

        over_steps(0, steps, 4, advance, half_of(after.at[0], block, groups), backward=True)
    copy.wait()


def grad_rows(tokens, groups, local_adjoints, shrink, weight, after_mine, after_other, partial, key, value, grad_query,
              grad_key, grad_value, grad_residue, grad_query_out,
              total, dense, factors, key_out, value_out, residue_out, sent, whole_sent):
    blocks = groups // SUB
    tiles = tokens // ROWS16

    pairs = ((key_out, grad_key), (value_out, grad_value))

    for block in range(blocks):
        rising, passed = powers(core_half(shrink, block, groups, False), core_half(weight, block, groups, False))
        for power, values in enumerate(rising + [passed]):
            for mode in range(HALF_MODES):
                factors[block, power, mode] = values[mode]

    def chunk(turn, states):
        tile = tiles - 1 - turn
        first = pl.multiple_of(tile * ROWS16, ROWS16)
        rows = pl.ds(first, ROWS16)
        states = [list(part) for part in states]
        for block in range(blocks):
            *rising, passed = [[factors[block, power, mode] for mode in range(HALF_MODES)] for power in range(STEP + 1)]
            for step in range(ROWS16 // STEP - 1, -1, -1):
                local = boundary(local_adjoints, block, tile * (ROWS16 // STEP) + step, tokens // STEP, False)
                behind = [s + e for s, e in zip(local, states[block])]
                for inner in range(STEP):
                    token = step * STEP + inner
                    part = tree_sum([w * s for w, s in zip(rising[STEP - 1 - inner], behind)])
                    part = part + partial[token_row(block, first + token, tokens), :]
                    dense[block, token * SUB : (token + 1) * SUB, :] = part
                states[block] = [p * e for p, e in zip(passed, states[block])]
            for group in range(block * SUB, (block + 1) * SUB):
                part = dense[block, pl.ds(group % SUB, ROWS16, stride=SUB), :]
                key_out[rows, lanes_of(group)] = (part * tile_of(value, first, group)).astype(bf16)
                value_out[rows, lanes_of(group)] = (part * tile_of(key, first, group)).astype(bf16)
        for copy in tile_copies(tile, sent, *pairs):
            copy.start()
        return states

    lax.fori_loop(0, tiles, chunk, [half_of(after_other.at[0], block, groups) for block in range(blocks)])
    half = HALF_MODES * groups
    core = lax.axis_index("core")
    total[my_rows(half), :] = after_mine[1]
    total[pl.ds(pl.multiple_of((1 - core) * half, half), half), :] = after_other[1]
    for group in range(groups):
        residue_out[:, lanes_of(group)] = total[pl.ds(group, MODES, stride=groups), :]
    whole_copies = [
        pltpu.make_async_copy(source, target, whole_sent.at[which])
        for which, (source, target) in enumerate(
            ((grad_query, grad_query_out), (residue_out, grad_residue))
        )
    ]
    for copy in whole_copies:
        copy.start()
    for tile in range(tiles):
        for copy in tile_copies(tile, sent, *pairs):
            copy.wait()
    for copy in whole_copies:
        copy.wait()


def swap(value, axis):
    return lax.ppermute(value, axis, [(0, 1), (1, 0)])


def on_device(query_rows, key_rows, value_rows, decay_rate, residue, norm_gain, grad_out):
    tokens, channels = query_rows.shape
    groups = channels // LANES
    half = HALF_MODES * groups
    chips = lax.axis_size(CHIP_AXES)
    cut = half // chips
    natural = shaped(tokens, channels, dtype=bf16)
    rates = shaped(MODES, channels)
    dense = shaped(tokens * groups + SUB, LANES)
    modal = shaped(2 * half + groups, LANES)
    halved = shaped(half, LANES)
    boundaries = shaped(tokens // STEP * 2 * half, LANES)
    two_halves = shaped(2, half, LANES)
    square = shaped(tokens, LANES)
    modal_scratch = pltpu.VMEM((2 * half + groups, LANES), f32)
    natural_scratch = pltpu.VMEM((tokens, channels), bf16)
    token_scratch = pltpu.VMEM((tokens * SUB + SUB, LANES), f32)
    bind = functools.partial

    inputs = (key_rows, value_rows, decay_rate, residue, norm_gain[None, :])
    product, local_states, keep, send, shrink, whole, key_near, value_near, rate_near, residue_near, gain = call(
        bind(local_ends, tokens, groups),
        (dense, boundaries, halved, halved, modal, halved, natural, natural, rates, rates, shaped(1, channels)),
        *[pltpu.with_memory_space_constraint(array, pltpu.HBM) for array in inputs],
        in_specs=[in_hbm] * len(inputs),
        scratch=[modal_scratch, pltpu.SemaphoreType.DMA((2 * len(CHUNKS) + 3,))],
    )
    whole_cut = whole.reshape(chips, cut, LANES)
    recv = swap(send, "core")
    asked, squared, weight, scale_dense = call(
        bind(prepare, tokens, groups), (dense, dense, modal, modal), query_rows, grad_out, gain, rate_near, residue_near
    )
    recv, asked = lax.optimization_barrier((recv, asked))
    total = call(chip_total, halved, whole, keep, recv)
    totals = lax.all_to_all(total.reshape(chips, cut, LANES), CHIP_AXES, 0, 0)
    before = call(bind(chip_scan, chips), shaped(chips, cut, LANES), whole_cut, totals)
    chip_state = lax.all_to_all(before, CHIP_AXES, 0, 0).reshape(half, LANES)
    entry_mine, entry_send = call(core_states, (halved, halved), whole, chip_state, keep, recv)
    entry_other = swap(entry_send, "core")

    partial = call(bind(filter_mine, tokens, groups), dense, product, local_states, shrink, weight, entry_mine)
    filtered, curved, sums = call(
        bind(filter_other, tokens, groups),
        (dense, dense, shaped(2, tokens)),
        local_states, shrink, weight, entry_other, partial, asked, squared,
        scratch=[token_scratch, token_scratch],
    )
    other_sums = swap(sums, "tp")
    product, sums = lax.optimization_barrier((product, sums))
    product_sums = call(bind(step_sums, tokens, groups), boundaries, product, shrink)

    inverse, slope, grad_filtered, local_adjoints, keep, send = call(
        bind(local_adjoint, tokens, groups),
        (square, square, dense, boundaries, two_halves, two_halves),
        sums, other_sums, asked, curved, product, product_sums, shrink, scale_dense, entry_mine, entry_other,
    )
    recv = swap(send, "core")
    normed_near, grad_query_near = call(
        bind(norm_rows, tokens, groups), (natural, natural), inverse, slope, filtered, query_rows, grad_out, gain
    )
    recv, normed_near, grad_query_near = lax.optimization_barrier((recv, normed_near, grad_query_near))
    total = call(bind(chip_total_and_sum, half, chips), shaped(chips, 2, cut, LANES), whole, keep, recv)
    totals = lax.all_to_all(total, CHIP_AXES, 0, 0)
    before = call(bind(chip_scan_and_sum, chips), shaped(chips, 2, cut, LANES), whole_cut, totals)
    chip_state = lax.all_to_all(before, CHIP_AXES, 0, 0)
    after_mine, after_send = call(
        bind(core_states_and_sum, half), (two_halves, two_halves), whole, chip_state, keep, recv
    )
    after_other = swap(after_send, "core")

    partial, normed_out = call(
        bind(grad_mine, tokens, groups),
        (dense, natural),
        grad_filtered, local_adjoints, shrink, weight, after_mine, normed_near,
        out_specs=(in_vmem, in_hbm),
        scratch=[pltpu.SemaphoreType.DMA],
    )
    grad_key, grad_value, grad_residue, grad_query = call(
        bind(grad_rows, tokens, groups),
        (natural, natural, rates, natural),
        local_adjoints, shrink, weight, after_mine, after_other, partial, key_near, value_near, grad_query_near,
        out_specs=(in_hbm,) * 4,
        scratch=[
            modal_scratch, pltpu.VMEM((groups // SUB, ROWS16 * SUB + SUB, LANES), f32),
            pltpu.VMEM((groups // SUB, STEP + 1, HALF_MODES, SUB, LANES), f32), natural_scratch, natural_scratch,
            pltpu.VMEM((MODES, channels), f32), pltpu.SemaphoreType.DMA((2, tokens // ROWS16)), pltpu.SemaphoreType.DMA((2,)),
        ],
    )
    return (normed_out, grad_query, grad_key, grad_value, grad_residue)


def solution(mesh):
    devices = mesh.devices
    cut_mesh = Mesh(devices.reshape(CTX_SIZES + (devices.shape[1],)), CTX_AXES + ("tp",))
    token_split = P(CTX_AXES, "tp")
    return jax.shard_map(
        on_device,
        mesh=cut_mesh,
        in_specs=(token_split, token_split, token_split, P(None, "tp"), P(None, "tp"), P("tp"), token_split),
        out_specs=(token_split, token_split, token_split, token_split, P(None, "tp")),
        check_vma=False,
    )
```
